32 devices in a mesh: groups: 2 (over x), lon: 8 (over z, y), lat: 2 (over core).
Axes of the slice: x: 2, y: 2, z: 4, core: 2. Of those that a mesh axis runs over, the one named last changes fastest.
Arguments:
- atmosphere: bfloat16 [256, 128, 512], P(('groups', 'lat'), 'lon'), parts along dimension 0, may hold values from -6 to 6
- pole_band: int32 [256], P(('groups', 'lat')), parts along dimension 0, may hold values from 0 to 15, never falling along the last dimension, each value on 1 to 96 neighbouring positions
- key_valid: int32 [256, 128], P(('groups', 'lat'), 'lon'), parts along dimension 0, may hold values 0 or 1
- norm_gains: float32 [2, 2, 512], replicated, may hold values from 0.5 to 1.5
- attend_in: bfloat16 [2, 512, 1536], replicated, as said below
- attend_out: bfloat16 [2, 512, 512], replicated, may hold values from -0.25 to 0.25
- expand: bfloat16 [2, 512, 1024], replicated, may hold values from -0.25 to 0.25
- contract: bfloat16 [2, 1024, 512], replicated, may hold values from -0.1875 to 0.1875
Outputs:
- evolved: bfloat16 [256, 128, 512], P(('groups', 'lat'), 'lon'), parts along dimension 0
The draws below stay inside these ranges and needn't reach their ends.
There are 2 independent parts, one for each index of `groups`. The reference program is written for one: setup_inputs(seed, part) draws one part's arguments, and reference() takes and returns one part's arrays. A program takes and returns all parts, laid end to end along the dimension named above; an argument that names none is the same for every part. Nothing has to cross between parts.
Inputs may be any that keep to these rules, and one draw needn't show every extreme that they name: `pole_band`: band numbers never fall along latitude, every number from 0 to the largest is used, and a band holds 1 to 96 rows. `attend_in`: query and value entries of order one over the square root of 512.
All inputs are finite; a program needn't handle non-finite values. No bound on the sum of `key_valid` on one device may be relied on, other than what follows from the above.
Results may differ from the reference program's by a relative error of at most 0.011.
Values may be sent and summed in bfloat16 or wider, within the bound.
No kernel may reach another device: no remote copies, remote signals or barrier semaphores. Data moves between devices by JAX's collectives and lax.ppermute only.
A program may use at most 128 MiB of HBM per device.

```python
import math
import jax
import jax.numpy as jnp
import numpy as np
from jax import lax

D = 512
H = 8
FF = 1024
WH = 32
WW = 16
LAYERS = 2
HD = 64
SH = 16
SW = 8
LAT = 128
LON = 128


def draw_attend_in(key, part):
    base = jax.random.truncated_normal(key, -3.0, 3.0, (LAYERS, D, 3 * D), jnp.float32) / math.sqrt(D)
    return base.astype(jnp.bfloat16)


def place_ends(values, key, least, largest):
    longest = values.shape.index(max(values.shape))
    spots = []
    for shift in (0, 1):
        where = [jax.random.randint(jax.random.fold_in(key, axis), (), 0, length) for axis, length in enumerate(values.shape)]
        where[longest] = (where[longest] + shift) % values.shape[longest]
        spots.append(tuple(where))
    return values.at[spots[0]].set(least).at[spots[1]].set(largest)


def levels(rng, dims, shards, least, top_value):
    factor_of, own = 1.0, jax.random.fold_in(rng, 6)
    for axis_at, blocks in shards:
        steps = jnp.exp(jax.random.uniform(jax.random.fold_in(own, axis_at), (blocks,), jnp.float32, least / len(shards), top_value / len(shards)))
        factor_of = factor_of * jnp.repeat(steps, dims[axis_at] // blocks).reshape([-1 if axis == axis_at else 1 for axis in range(len(dims))])
    return factor_of


def profile(count, total, limit, lean):
    loads = [(1 << 20) // math.isqrt(rank ** lean) + 1 for rank in range(2, count + 1)]
    spare, given = total - limit - (count - 1), [1] * (count - 1)
    while spare > 0:
        movable = [i for i in range(count - 1) if given[i] < limit]
        whole, budget = sum([loads[i] for i in movable]), spare
        for i in movable:
            more = min(limit - given[i], max(1, budget * loads[i] // whole), spare)
            given[i] = given[i] + more
            spare = spare - more
    return np.array([limit] + given)


def ragged(stream_key, count, total, bound, skew):
    if count == 2:
        one = jax.random.randint(stream_key, (), max(1, total - bound), min(bound, total - 1) + 1)
        return jnp.stack([one, total - one])
    lengths = jnp.asarray(profile(count, total, bound, skew), jnp.int32)
    twos = (count - 1) // 2
    giver, sink = lengths[1:1 + 2 * twos:2], lengths[2:2 + 2 * twos:2]
    room = jnp.minimum(giver - 1, bound - sink)
    moved = jax.random.randint(jax.random.fold_in(stream_key, 1), (twos,), 0, 1 << 20) % (room + 1)
    lengths = lengths.at[1:1 + 2 * twos:2].set(giver - moved).at[2:2 + 2 * twos:2].set(sink + moved)
    return lengths[jax.random.permutation(jax.random.fold_in(stream_key, 2), count)]


def gaussian(stream_key, dims, scale, reach, pieces=(), held_as=jnp.bfloat16):
    loudness = levels(stream_key, dims, pieces, -0.22, 0.18) if pieces else 1.0
    drawn = jax.random.normal(stream_key, dims, jnp.float32) * scale * loudness
    return jnp.minimum(jnp.maximum(drawn, -reach), reach).astype(held_as)


def setup_inputs(seed: int = 0, part: int = 0) -> dict:
    streams_of = jax.random.split(jax.random.key(seed), 9)
    part_splits = jax.random.split(jax.random.fold_in(streams_of[8], part), 9)
    return {
        "atmosphere": gaussian(part_splits[0], (LAT, LON, D), 1.0, 6.0, ((0, 2), (1, 8))),
        "pole_band": jnp.searchsorted(jnp.cumsum(ragged(part_splits[1], max(2, LAT // 8), LAT, 3 * LAT // 4, 0)), jnp.arange(LAT), side="right").astype(jnp.int32),
        "key_valid": place_ends((jax.random.randint(part_splits[2], (LAT, LON), 0, 4) < 3).astype(jnp.int32), jax.random.fold_in(part_splits[2], 1), 0, 1),
        "norm_gains": jnp.clip(1.0 + 0.1 * jax.random.normal(streams_of[3], (LAYERS, 2, D), jnp.float32), 0.5, 1.5),
        "attend_in": draw_attend_in(jax.random.fold_in(streams_of[8], 71), part),
        "attend_out": gaussian(streams_of[5], (LAYERS, D, D), D ** -0.5, 0.25),
        "expand": gaussian(streams_of[6], (LAYERS, D, FF), D ** -0.5, 0.25),
        "contract": gaussian(streams_of[7], (LAYERS, FF, D), FF ** -0.5, 0.1875),
    }


norm_eps = 1e-05

def normalize(field, gains):
    widened = field.astype(jnp.float32)
    average = lax.optimization_barrier(jnp.mean(widened, -1, keepdims=True))
    centred = widened - average
    spread = lax.optimization_barrier(jnp.mean(centred * centred, -1, keepdims=True))
    return (centred * lax.rsqrt(spread + norm_eps) * gains).astype(jnp.bfloat16)

def windows_of(field):
    height, breadth = (field.shape[0], field.shape[1])
    rest = field.shape[2:]
    tiles = field.reshape((height // WH, WH, breadth // WW, WW) + rest)
    return jnp.swapaxes(tiles, 1, 2).reshape((-1, WH * WW) + rest)

def field_of(tiles, height, breadth):
    rest = tiles.shape[2:]
    grid = tiles.reshape((height // WH, breadth // WW, WH, WW) + rest)
    return jnp.swapaxes(grid, 1, 2).reshape((height, breadth) + rest)

def attend_window(packed, bands, masks):
    cells = packed.shape[0]
    heads = packed.reshape(cells, 3, H, HD).astype(jnp.float32)
    queries = heads[:, 0]
    keyed = heads[:, 1]
    valued = heads[:, 2]
    scores = jnp.einsum('qhd,khd->hqk', queries, keyed) * (1.0 / math.sqrt(HD))
    itself = jnp.arange(cells)[:, None] == jnp.arange(cells)[None, :]
    allowed = (bands[:, None] == bands[None, :]) & ((masks[None, :] == 1) | itself)
    scores = jnp.where(allowed[None], scores, -1e+30)
    row_max = lax.optimization_barrier(jnp.max(scores, -1, keepdims=True))
    raw_weights = jnp.exp(scores - row_max)
    probs = (raw_weights / lax.optimization_barrier(jnp.sum(raw_weights, -1, keepdims=True))).astype(jnp.bfloat16)
    context = jnp.einsum('hqk,khd->qhd', probs.astype(jnp.float32), valued)
    return context.astype(jnp.bfloat16).reshape(cells, D)

def layer(field, bands, masks, index, norm_gains, attend_in, attend_out, expand, contract):
    height, breadth = (field.shape[0], field.shape[1])
    normed = normalize(field, norm_gains[index, 0]).reshape(-1, D)
    projected = jnp.dot(normed, attend_in[index], preferred_element_type=jnp.float32)
    projected = projected.astype(jnp.bfloat16).reshape(height, breadth, 3 * D)
    band_grid = jnp.broadcast_to(bands[:, None], (height, breadth))
    context = lax.map(lambda item: attend_window(item[0], item[1], item[2]), (windows_of(projected), windows_of(band_grid), windows_of(masks)))
    context = field_of(context, height, breadth).reshape(-1, D)
    resid = field.reshape(-1, D).astype(jnp.float32) + jnp.dot(context, attend_out[index], preferred_element_type=jnp.float32)
    resid = resid.astype(jnp.bfloat16)
    normed_mlp = normalize(resid, norm_gains[index, 1])
    hidden = jax.nn.gelu(jnp.dot(normed_mlp, expand[index], preferred_element_type=jnp.float32), approximate=True)
    hidden = hidden.astype(jnp.bfloat16)
    layer_out = resid.astype(jnp.float32) + jnp.dot(hidden, contract[index], preferred_element_type=jnp.float32)
    return layer_out.astype(jnp.bfloat16).reshape(height, breadth, D)

def reference(atmosphere, pole_band, key_valid, norm_gains, attend_in, attend_out, expand, contract):
    shifted = jnp.roll(atmosphere, (-SH, -SW), axis=(0, 1))
    shifted_band = jnp.roll(pole_band, -SH)
    shifted_valid = jnp.roll(key_valid, (-SH, -SW), axis=(0, 1))
    first = layer(shifted, shifted_band, shifted_valid, 0, norm_gains, attend_in, attend_out, expand, contract)
    back = jnp.roll(first, (SH, SW), axis=(0, 1))
    return layer(back, pole_band, key_valid, 1, norm_gains, attend_in, attend_out, expand, contract)
```

```python
import functools
import math

import jax
import jax.numpy as jnp
from jax import lax
from jax.experimental import pallas as pl
from jax.experimental.pallas import tpu as pltpu
from jax.sharding import PartitionSpec as P

D = 512
H = 8
WH = 32
WW = 16
HD = 64
SH = 16
SW = 8

norm_eps = 1e-05

F32 = jnp.float32
BF16 = jnp.bfloat16
CLASSES = 128
META = 16
QSCALE = math.log2(math.e) / math.sqrt(HD)
TRANSPOSED_RIGHT = (((1,), (1,)), ((), ()))
TRANSPOSED_LEFT = (((0,), (0,)), ((), ()))
VMEM = pl.BlockSpec(memory_space=pltpu.VMEM)
SMEM = pl.BlockSpec(memory_space=pltpu.SMEM)


def product(left, right):
    return jnp.dot(left, right, preferred_element_type=F32)


def normalize(field, gains):
    average = jnp.mean(field, -1, keepdims=True)
    centred = field - average
    spread = jnp.mean(centred * centred, -1, keepdims=True)
    return (centred * lax.rsqrt(spread + norm_eps) * gains).astype(BF16)


def gelu(value):
    inner = math.sqrt(2.0 / math.pi) * (value + 0.044715 * value * value * value)
    return 0.5 * value * (1.0 + jnp.tanh(inner))


def half_columns(block, start):
    part = block.astype(F32)[:, start : start + SW]
    return part.reshape(block.shape[0] * SW, D)


def mask_lanes(valid, start, lanes):
    rows = valid.shape[0]
    column = lax.broadcasted_iota(jnp.int32, (valid.shape[1], lanes), 0)
    cell = lax.broadcasted_iota(jnp.int32, (valid.shape[1], lanes), 1)
    pick = (column == start + lax.rem(cell, SW)).astype(F32).astype(BF16)
    spread = product(valid.astype(F32).astype(BF16), pick)
    row = lax.broadcasted_iota(jnp.int32, (rows, lanes), 0)
    own = lax.div(lax.broadcasted_iota(jnp.int32, (rows, lanes), 1), SW)
    return jnp.sum(jnp.where(row == own, spread, 0.0), 0, keepdims=True)


def band_lanes(bands, start, rows, lanes):
    own = lax.div(lax.broadcasted_iota(jnp.int32, (1, lanes), 1), SW)
    found = jnp.zeros((1, lanes), jnp.int32)
    for row in range(rows):
        found = jnp.where(own == row, bands[start + row], found)
    return found.astype(F32)


def meta_rows(masks, bands):
    row = lax.broadcasted_iota(jnp.int32, (META, masks.shape[1]), 0)
    return jnp.where(row == 0, masks, jnp.where(row == 1, bands, 0.0)).astype(BF16)


def meta_of(ref, cells):
    tail = ref[pl.ds(cells, META), :].astype(F32)
    return tail[0:1, :cells], tail[1:2, :cells]


def project(field, gain, attend_in, at, query, key, value):
    rows = pl.ds(at, field.shape[0])
    normed = normalize(field, gain)
    query[rows, :] = (product(normed, attend_in[:, :D]) * QSCALE).astype(BF16)
    key[rows, :] = product(normed, attend_in[:, D : 2 * D]).astype(BF16)
    value[rows, :] = product(normed, attend_in[:, 2 * D :]).astype(BF16)


def set_bias(bias, bands, masks):
    cells = bands.shape[1]
    classes = lax.broadcasted_iota(jnp.int32, (CLASSES, cells), 0).astype(F32)
    one_hot = (classes == bands).astype(F32).astype(BF16)
    same = lax.dot_general(one_hot, one_hot, TRANSPOSED_LEFT, preferred_element_type=F32)
    asking = lax.broadcasted_iota(jnp.int32, (cells, cells), 0)
    asked = lax.broadcasted_iota(jnp.int32, (cells, cells), 1)
    allowed = (same > 0.5) & ((masks > 0.5) | (asking == asked))
    bias[...] = jnp.where(allowed, 0.0, -1e30)


def attend(query, key, value, bias, context):
    first = lax.broadcasted_iota(jnp.int32, (1, 2 * HD), 1) < HD
    for pair in range(H // 2):
        lanes = slice(2 * HD * pair, 2 * HD * (pair + 1))
        queries, keys, values = query[:, lanes], key[:, lanes], value[:, lanes]
        zero, one = jnp.zeros_like(queries), jnp.ones_like(values)
        sides = (
            (jnp.where(first, queries, zero), jnp.where(first, values, one)),
            (jnp.where(first, zero, queries), jnp.where(first, one, values)),
        )
        sums = []
        for own_queries, own_values in sides:
            scores = lax.dot_general(
                own_queries, keys, TRANSPOSED_RIGHT, preferred_element_type=F32
            )
            scores = scores + bias[...]
            row_max = jnp.max(scores, -1, keepdims=True)
            weights = jnp.exp2(scores - row_max).astype(BF16)
            sums.append(product(weights, own_values))
        above = jnp.where(first, sums[0], sums[1])
        below = pltpu.roll(jnp.where(first, sums[1], sums[0]), HD, 1)
        context[:, lanes] = (above / below).astype(BF16)


def finish(field, context, attend_out, gain, expand, contract):
    resid = (field + product(context, attend_out)).astype(BF16).astype(F32)
    normed = normalize(resid, gain)
    hidden = gelu(product(normed, expand)).astype(BF16)
    return resid + product(hidden, contract)


def pack_kernel(block, bands, valid, main, side, corner, row_end):
    height = block.shape[0]
    places = ((main, SH, height - SH, 0), (side, height - SH, height, 0),
              (corner, 0, SH, 0), (row_end, 0, SH, SW))
    for out, low, high, column in places:
        cells = (high - low) * SW
        out[pl.ds(0, cells), :] = half_columns(block[low:high], column).astype(BF16)
        masks = mask_lanes(valid[low:high], column, D)
        out[pl.ds(cells, META), :] = meta_rows(masks, band_lanes(bands, low, high - low, D))


def window_a_kernel(
    block, bands, valid, taken, gains, attend_in, attend_out, expand, contract,
    away, home, query, key, value, bias, context,
):
    height = block.shape[0]
    rows = height - 2 * SH
    cells = rows * SW
    local = half_columns(block[SH : SH + rows], SW)
    remote = taken[pl.ds(0, cells), :].astype(F32)
    project(local, gains[0:1], attend_in, 0, query, key, value)
    project(remote, gains[0:1], attend_in, cells, query, key, value)
    row_bands = band_lanes(bands, SH, rows, cells)
    masks, _ = meta_of(taken, cells)
    set_bias(
        bias,
        jnp.concatenate([row_bands, row_bands], 1),
        jnp.concatenate([mask_lanes(valid[SH : SH + rows], SW, cells), masks], 1),
    )
    attend(query, key, value, bias, context)
    field = jnp.concatenate([local, remote], 0)
    out = finish(field, context[...], attend_out[...], gains[1:2], expand[...], contract[...])
    out = out.astype(BF16)
    home[...] = out[:cells]
    away[...] = out[cells:]


def window_b_kernel(
    block, bands, valid, taken_side, taken_corner, taken_end,
    gains, attend_in, attend_out, expand, contract,
    away_side, away_corner, home_side, home_end, query, key, value, bias, context,
):
    height = block.shape[0]
    cells = SH * SW
    parts = [half_columns(block[height - SH :], SW)]
    bands_here = [band_lanes(bands, height - SH, SH, cells)]
    masks_here = [mask_lanes(valid[height - SH :], SW, cells)]
    for taken in (taken_end, taken_side, taken_corner):
        parts.append(taken[pl.ds(0, cells), :].astype(F32))
        masks, row_bands = meta_of(taken, cells)
        masks_here.append(masks)
        bands_here.append(row_bands)
    field = jnp.concatenate(parts, 0)
    project(field, gains[0:1], attend_in, 0, query, key, value)
    set_bias(bias, jnp.concatenate(bands_here, 1), jnp.concatenate(masks_here, 1))
    attend(query, key, value, bias, context)
    out = finish(field, context[...], attend_out[...], gains[1:2], expand[...], contract[...])
    out = out.astype(BF16)
    for index, ref in enumerate((home_side, home_end, away_side, away_corner)):
        ref[...] = out[index * cells : (index + 1) * cells]


def second_kernel(
    home, home_side, near_end, far, far_side, far_corner, bands, valid,
    gains, attend_in, attend_out, expand, contract,
    out_ref, query, key, value, bias, context,
):
    half = SH * SW
    low, high = pl.ds(0, half), pl.ds(half, half)
    windows = (
        (near_end[...], home[low, :], far_corner[...], far[low, :]),
        (home[high, :], home_side[...], far[high, :], far_side[...]),
    )
    for index, parts in enumerate(windows):
        field = jnp.concatenate([part.astype(F32) for part in parts], 0)
        project(field, gains[0:1], attend_in, 0, query, key, value)
        rows = slice(index * WH, (index + 1) * WH)
        row_bands = band_lanes(bands, index * WH, WH, 2 * half)
        set_bias(
            bias,
            jnp.concatenate([row_bands, row_bands], 1),
            jnp.concatenate(
                [mask_lanes(valid[rows], SW, 2 * half), mask_lanes(valid[rows], 0, 2 * half)], 1
            ),
        )
        attend(query, key, value, bias, context)
        out = finish(field, context[...], attend_out[...], gains[1:2], expand[...], contract[...])
        right = out[: 2 * half].reshape(WH, SW, D)
        left = out[2 * half :].reshape(WH, SW, D)
        out_ref[pl.ds(index * WH, WH)] = jnp.concatenate([left, right], 1).astype(BF16)


def call(kernel, name, shapes, specs, scratch, flops, *operands):
    size = sum(operand.size * operand.dtype.itemsize for operand in operands)
    return pl.pallas_call(
        kernel,
        out_shape=[jax.ShapeDtypeStruct(shape, BF16) for shape in shapes],
        in_specs=specs,
        out_specs=[VMEM] * len(shapes),
        scratch_shapes=scratch,
        compiler_params=pltpu.CompilerParams(vmem_limit_bytes=40 * 2**20),
        cost_estimate=pl.CostEstimate(flops=flops, bytes_accessed=size, transcendentals=0),
        name=name,
    )(*operands)


def on_device(
    atmosphere, pole_band, key_valid, norm_gains, attend_in, attend_out, expand, contract
):
    height, breadth = atmosphere.shape[0], atmosphere.shape[1]
    assert height == 2 * WH and breadth == WW
    lons, lats = lax.axis_size("lon"), lax.axis_size("lat")

    def moved(value, lon_step, lat_step):
        pairs = [
            (lon * lats + lat, (lon + lon_step) % lons * lats + (lat + lat_step) % lats)
            for lon in range(lons)
            for lat in range(lats)
        ]
        return lax.ppermute(value, ("lon", "lat"), pairs)

    cells = WH * WW
    quarter = cells // 4
    scratch = (
        [pltpu.VMEM((cells, D), BF16)] * 3
        + [pltpu.VMEM((cells, cells), F32), pltpu.VMEM((cells, D), BF16)]
    )
    hidden = expand.shape[-1]
    flops = 2 * cells * D * (4 * D + 2 * hidden) + 4 * cells * cells * D

    main, side, corner, row_end = call(
        pack_kernel, "pack",
        [(2 * quarter + META, D)] + [(quarter + META, D)] * 3,
        [VMEM, SMEM, VMEM], [], 10**6, atmosphere, pole_band, key_valid,
    )
    far_main = moved(main, -1, 0)
    far_side = moved(side, -1, 0)
    far_corner = moved(corner, -1, -1)
    near_end = moved(row_end, 0, -1)

    layer_weights = [
        (norm_gains[k], attend_in[k], attend_out[k], expand[k], contract[k]) for k in range(2)
    ]
    place = (atmosphere, pole_band, key_valid)
    where = [VMEM, SMEM, VMEM]
    away, home = call(
        window_a_kernel, "window_a", [(2 * quarter, D)] * 2, where + [VMEM] * 6, scratch, flops,
        *place, far_main, *layer_weights[0],
    )
    back_main = moved(away, 1, 0)
    away_side, away_corner, home_side, home_end = call(
        window_b_kernel, "window_b", [(quarter, D)] * 4, where + [VMEM] * 8, scratch, flops,
        *place, far_side, far_corner, near_end, *layer_weights[0],
    )
    back_side = moved(away_side, 1, 0)
    back_corner = moved(away_corner, 1, 1)
    back_end = moved(home_end, 0, 1)
    return call(
        second_kernel, "second", [(height, breadth, D)],
        [VMEM] * 6 + [SMEM] + [VMEM] * 6, scratch, 2 * flops,
        home, home_side, back_end, back_main, back_side, back_corner,
        pole_band, key_valid, *layer_weights[1],
    )[0]


def solution(mesh):
    in_specs = (
        P(("groups", "lat"), "lon", None),
        P(("groups", "lat")),
        P(("groups", "lat"), "lon"),
        P(),
        P(),
        P(),
        P(),
        P(),
    )
    out_specs = P(("groups", "lat"), "lon", None)
    return jax.shard_map(
        on_device, mesh=mesh, in_specs=in_specs, out_specs=out_specs, check_vma=False
    )
```

```python
import functools
import math

import jax
import jax.numpy as jnp
from jax import lax
from jax.experimental import pallas as pl
from jax.experimental.pallas import tpu as pltpu
from jax.sharding import PartitionSpec as P

D = 512
H = 8
WH = 32
WW = 16
HD = 64
SH = 16
SW = 8

norm_eps = 1e-05

F32 = jnp.float32
BF16 = jnp.bfloat16
CLASSES = 128
META = 16
QSCALE = math.log2(math.e) / math.sqrt(HD)
TRANSPOSED_RIGHT = (((1,), (1,)), ((), ()))
TRANSPOSED_LEFT = (((0,), (0,)), ((), ()))
VMEM = pl.BlockSpec(memory_space=pltpu.VMEM)
SMEM = pl.BlockSpec(memory_space=pltpu.SMEM)
HBM = pl.BlockSpec(memory_space=pltpu.HBM)


def product(left, right):
    return jnp.dot(left, right, preferred_element_type=F32)


def normalize(field, gains):
    average = jnp.mean(field, -1, keepdims=True)
    centred = field - average
    spread = jnp.mean(centred * centred, -1, keepdims=True)
    return (centred * lax.rsqrt(spread + norm_eps) * gains).astype(BF16)


def gelu(value):
    scale = math.sqrt(2.0 / math.pi)
    bent = jnp.tanh(value * (scale + (scale * 0.044715) * (value * value)))
    half = 0.5 * value
    return half + half * bent


def half_columns(block, start):
    part = block.astype(F32)[:, start : start + SW]
    return part.reshape(block.shape[0] * SW, D)


def mask_lanes(valid, low, start, lanes):
    columns, height = valid.shape
    row = lax.broadcasted_iota(jnp.int32, (height, lanes), 0)
    cell = lax.broadcasted_iota(jnp.int32, (height, lanes), 1)
    pick = (row == low + lax.div(cell, SW)).astype(F32).astype(BF16)
    spread = product(valid[...].astype(F32).astype(BF16), pick)
    column = lax.broadcasted_iota(jnp.int32, (columns, lanes), 0)
    own = start + lax.rem(lax.broadcasted_iota(jnp.int32, (columns, lanes), 1), SW)
    return jnp.sum(jnp.where(column == own, spread, 0.0), 0, keepdims=True)


def band_lanes(bands, start, rows, lanes):
    own = lax.div(lax.broadcasted_iota(jnp.int32, (1, lanes), 1), SW)
    found = jnp.zeros((1, lanes), jnp.int32)
    for row in range(rows):
        found = jnp.where(own == row, bands[start + row], found)
    return found.astype(F32)


def meta_rows(masks, bands):
    row = lax.broadcasted_iota(jnp.int32, (META, masks.shape[1]), 0)
    return jnp.where(row == 0, masks, jnp.where(row == 1, bands, 0.0)).astype(BF16)


def meta_of(ref, cells):
    tail = ref[pl.ds(cells, META), :].astype(F32)
    return tail[0:1, :cells], tail[1:2, :cells]


def in_turn(count, stages):
    state = [None] * count
    for step in range(count + len(stages) - 1):
        for index, stage in enumerate(stages):
            piece = step - index
            if 0 <= piece < count:
                state[piece] = stage(piece, state[piece])


def project(field, gain, attend_in, at, query, key, value):
    rows = pl.ds(at, field.shape[0])
    normed = normalize(field, gain)
    query[rows, :] = (product(normed, attend_in[:, :D]) * QSCALE).astype(BF16)
    key[rows, :] = product(normed, attend_in[:, D : 2 * D]).astype(BF16)
    value[rows, :] = product(normed, attend_in[:, 2 * D :]).astype(BF16)


def set_bias(bias, bands, masks):
    cells = bands.shape[1]
    classes = lax.broadcasted_iota(jnp.int32, (CLASSES, cells), 0).astype(F32)
    one_hot = (classes == bands).astype(F32).astype(BF16)
    same = lax.dot_general(one_hot, one_hot, TRANSPOSED_LEFT, preferred_element_type=F32)
    asking = lax.broadcasted_iota(jnp.int32, (cells, cells), 0)
    asked = lax.broadcasted_iota(jnp.int32, (cells, cells), 1)
    allowed = (same > 0.5) & ((masks > 0.5) | (asking == asked))
    bias[...] = jnp.where(allowed, 0.0, -1e30)


def attend(query, key, value, bias, context, low, count):
    first = lax.broadcasted_iota(jnp.int32, (1, 2 * HD), 1) < HD
    rows = pl.ds(low, count)
    sums = {}

    def lanes(unit):
        return slice(2 * HD * (unit // 2), 2 * HD * (unit // 2 + 1))

    def own(unit, inside, outside):
        return jnp.where(first, inside, outside) if unit % 2 == 0 else jnp.where(first, outside, inside)

    def score(unit, _):
        queries = query[rows, lanes(unit)]
        queries = own(unit, queries, jnp.zeros_like(queries))
        scores = lax.dot_general(
            queries, key[:, lanes(unit)], TRANSPOSED_RIGHT, preferred_element_type=F32
        )
        return scores + bias[rows, :]

    def weigh(unit, scores):
        return jnp.exp2(scores - jnp.max(scores, -1, keepdims=True)).astype(BF16)

    def gather(unit, weights):
        values = value[:, lanes(unit)]
        sums[unit] = product(weights, own(unit, values, jnp.ones_like(values)))
        if unit % 2 == 1:
            even, odd = sums.pop(unit - 1), sums.pop(unit)
            above = jnp.where(first, even, odd)
            below = pltpu.roll(jnp.where(first, odd, even), HD, 1)
            context[rows, lanes(unit)] = (above / below).astype(BF16)

    in_turn(H, (score, weigh, gather))


def finish(fields, context, low, piece, attend_out, gain, expand, contract, write):
    def start(index, _):
        rows = pl.ds(low + index * piece, piece)
        added = fields[index] + product(context[rows, :], attend_out[...])
        resid = added.astype(BF16).astype(F32)
        return resid, normalize(resid, gain)

    def widen(index, state):
        return state[0], product(state[1], expand[...])

    def bend(index, state):
        return state[0], gelu(state[1]).astype(BF16)

    def end(index, state):
        write(index, state[0] + product(state[1], contract[...]))

    in_turn(len(fields), (start, widen, bend, end))


def pack_main_kernel(block_hbm, valid_hbm, main, block, valid, sems):
    height = block_hbm.shape[0]
    rows = height - 2 * SH
    copies = (
        pltpu.make_async_copy(valid_hbm, valid, sems.at[0]),
        pltpu.make_async_copy(block_hbm.at[pl.ds(SH, rows)], block, sems.at[1]),
    )
    for copy in copies:
        copy.start()
    copies[0].wait()
    masks = mask_lanes(valid, SH, 0, D)
    main[pl.ds(rows * SW, META), :] = meta_rows(masks, jnp.zeros_like(masks))
    copies[1].wait()
    main[pl.ds(0, rows * SW), :] = half_columns(block[...], 0).astype(BF16)


def early_kernel(
    block, bands, valid, main, gains, attend_in,
    side, corner, row_end, query, key, value,
):
    height = block.shape[0]
    rows = height - 2 * SH
    places = ((side, height - SH, 0), (corner, 0, 0), (row_end, 0, SW))
    for out, low, column in places:
        cells = SH * SW
        out[pl.ds(0, cells), :] = half_columns(block[low : low + SH], column).astype(BF16)
        masks = mask_lanes(valid, low, column, D)
        out[pl.ds(cells, META), :] = meta_rows(masks, band_lanes(bands, low, SH, D))
    local = half_columns(block[SH:], SW)
    project(local, gains[0:1], attend_in, 0, query, key, value)


def window_a_kernel(
    block, bands, valid, taken, near_query, near_key, near_value,
    gains, attend_in, attend_out, expand, contract,
    away, home, query, key, value, bias, context,
):
    height = block.shape[0]
    rows = height - 2 * SH
    cells = rows * SW
    for near, whole in ((near_query, query), (near_key, key), (near_value, value)):
        whole[pl.ds(0, cells), :] = near[pl.ds(0, cells), :]
    local = half_columns(block[SH : SH + rows], SW)
    remote = taken[pl.ds(0, cells), :].astype(F32)
    project(remote, gains[0:1], attend_in, cells, query, key, value)
    row_bands = band_lanes(bands, SH, rows, cells)
    masks, _ = meta_of(taken, cells)
    set_bias(
        bias,
        jnp.concatenate([row_bands, row_bands], 1),
        jnp.concatenate([mask_lanes(valid, SH, SW, cells), masks], 1),
    )
    attend(query, key, value, bias, context, 0, 2 * cells)

    def write(index, out):
        (home, away)[index][...] = out.astype(BF16)

    finish([local, remote], context, 0, cells, attend_out, gains[1:2], expand, contract, write)


def window_b_away_kernel(
    bands, valid, taken_side, taken_corner, taken_end, near_query, near_key, near_value,
    gains, attend_in, attend_out, expand, contract,
    away_side, away_corner, query, key, value, bias, context,
):
    height = bands.shape[0]
    cells = SH * SW
    for near, whole in ((near_query, query), (near_key, key), (near_value, value)):
        whole[pl.ds(0, cells), :] = near[pl.ds(near.shape[0] - cells, cells), :]
    fields = []
    bands_here = [band_lanes(bands, height - SH, SH, cells)]
    masks_here = [mask_lanes(valid, height - SH, SW, cells)]
    for taken in (taken_end, taken_side, taken_corner):
        fields.append(taken[pl.ds(0, cells), :].astype(F32))
        masks, row_bands = meta_of(taken, cells)
        masks_here.append(masks)
        bands_here.append(row_bands)
    project(jnp.concatenate(fields, 0), gains[0:1], attend_in, cells, query, key, value)
    set_bias(bias, jnp.concatenate(bands_here, 1), jnp.concatenate(masks_here, 1))
    attend(query, key, value, bias, context, 2 * cells, 2 * cells)

    def write(index, out):
        (away_side, away_corner)[index][...] = out.astype(BF16)

    finish(fields[1:], context, 2 * cells, cells, attend_out, gains[1:2], expand, contract, write)


def window_b_home_kernel(
    block, taken_end, query, key, value, bias, gains, attend_out, expand, contract,
    home_side, home_end, context,
):
    height = block.shape[0]
    cells = SH * SW
    attend(query, key, value, bias, context, 0, 2 * cells)
    fields = [half_columns(block[height - SH :], SW), taken_end[pl.ds(0, cells), :].astype(F32)]

    def write(index, out):
        (home_side, home_end)[index][...] = out.astype(BF16)

    finish(fields, context, 0, cells, attend_out, gains[1:2], expand, contract, write)


def second_early_kernel(
    home, home_side, near_end, far, bands, valid, gains, attend_in,
    query, key, value, bias,
):
    part = SH * SW
    low, high = slice(0, part), slice(part, 2 * part)
    windows = ((near_end[...], home[low], far[low]), (home[high], home_side[...], far[high]))
    for index, parts in enumerate(windows):
        field = jnp.concatenate([piece.astype(F32) for piece in parts], 0)
        project(field, gains[0:1], attend_in, 0, query.at[index], key.at[index], value.at[index])
        row = index * WH
        row_bands = band_lanes(bands, row, WH, 2 * part)
        near_masks = mask_lanes(valid, row, SW, 2 * part)
        far_masks = mask_lanes(valid, row, 0, 2 * part)
        far_bands = row_bands
        if index == 0:
            far_bands = jnp.concatenate([row_bands[:, part:], row_bands[:, :part]], 1)
            far_masks = jnp.concatenate([far_masks[:, part:], far_masks[:, :part]], 1)
        set_bias(
            bias.at[index],
            jnp.concatenate([row_bands, far_bands], 1),
            jnp.concatenate([near_masks, far_masks], 1),
        )


def second_kernel(
    home, home_side, near_end, far, far_side, far_corner,
    early_query, early_key, early_value, bias,
    gains, attend_in, attend_out, expand, contract,
    out_ref, query, key, value, context,
):
    part = SH * SW
    low, high = slice(0, part), slice(part, 2 * part)
    windows = (
        (near_end[...], home[low], far[low], far_corner[...]),
        (home[high], home_side[...], far[high], far_side[...]),
    )
    windows = [[piece.astype(F32) for piece in parts] for parts in windows]
    late = 3 * part
    for early, whole in ((early_query, query), (early_key, key), (early_value, value)):
        whole[:, pl.ds(0, late), :] = early[:, pl.ds(0, late), :]
    for index, parts in enumerate(windows):
        project(parts[3], gains[0:1], attend_in, late, query.at[index], key.at[index], value.at[index])
    for index in range(len(windows)):
        attend(
            query.at[index], key.at[index], value.at[index], bias.at[index],
            context.at[pl.ds(4 * part * index, 4 * part)], 0, 4 * part,
        )
    fields = [jnp.concatenate(parts[at : at + 2], 0) for parts in windows for at in (0, 2)]
    near = {}

    def write(index, out):
        window = index // 2
        if index % 2 == 0:
            near[window] = out
            return
        if window == 0:
            out = jnp.concatenate([out[part:], out[:part]], 0)
        both = [piece.reshape(WH, SW, D) for piece in (out, near.pop(window))]
        out_ref[pl.ds(window * WH, WH)] = jnp.concatenate(both, 1).astype(BF16)

    finish(fields, context, 0, 2 * part, attend_out, gains[1:2], expand, contract, write)


def call(kernel, name, shapes, specs, scratch, flops, *operands, limit=40):
    size = sum(operand.size * operand.dtype.itemsize for operand in operands)
    shapes = [shape if isinstance(shape, jax.ShapeDtypeStruct) else jax.ShapeDtypeStruct(shape, BF16)
              for shape in shapes]
    return pl.pallas_call(
        kernel,
        out_shape=shapes,
        in_specs=specs,
        out_specs=[VMEM] * len(shapes),
        scratch_shapes=scratch,
        compiler_params=pltpu.CompilerParams(vmem_limit_bytes=limit * 2**20),
        cost_estimate=pl.CostEstimate(flops=flops, bytes_accessed=size, transcendentals=0),
        name=name,
    )(*operands)


def on_device(
    atmosphere, pole_band, key_valid, norm_gains, attend_in, attend_out, expand, contract
):
    height, breadth = atmosphere.shape[0], atmosphere.shape[1]
    assert height == 2 * WH and breadth == WW
    lons, lats = lax.axis_size("lon"), lax.axis_size("lat")

    def moved(value, lon_step, lat_step):
        pairs = [
            (lon * lats + lat, (lon + lon_step) % lons * lats + (lat + lat_step) % lats)
            for lon in range(lons)
            for lat in range(lats)
        ]
        return lax.ppermute(value, ("lon", "lat"), pairs)

    cells = WH * WW
    half, quarter = cells // 2, cells // 4
    wide = pltpu.VMEM((cells, D), BF16)
    bias_shape = jax.ShapeDtypeStruct((cells, cells), F32)
    bias_scratch = pltpu.VMEM((cells, cells), F32)
    hidden = expand.shape[-1]
    each = 2 * D * 3 * D
    flops = cells * 2 * D * (D + 2 * hidden) + 4 * cells * cells * D

    valid = key_valid.T
    main = call(
        pack_main_kernel, "pack_main", [(half + META, D)], [HBM] * 2,
        [pltpu.VMEM((WH, breadth, D), BF16), pltpu.VMEM(valid.shape, valid.dtype),
         pltpu.SemaphoreType.DMA((2,))],
        10**6, atmosphere, valid, limit=62,
    )[0]
    far_main = moved(main, -1, 0)

    weights = [
        (norm_gains[k], attend_in[k], attend_out[k], expand[k], contract[k]) for k in range(2)
    ]
    side, corner, row_end, *near = call(
        early_kernel, "early", [(quarter + META, D)] * 3 + [(half + quarter, D)] * 3,
        [VMEM, SMEM] + [VMEM] * 4, [], each * (half + quarter),
        atmosphere, pole_band, valid, main, *weights[0][:2],
    )
    far_side = moved(side, -1, 0)
    far_corner = moved(corner, -1, -1)
    near_end = moved(row_end, 0, -1)

    away, home = call(
        window_a_kernel, "window_a", [(half, D)] * 2, [VMEM, SMEM] + [VMEM] * 10,
        [wide] * 3 + [bias_scratch, wide], flops + each * half,
        atmosphere, pole_band, valid, far_main, *near, *weights[0],
    )
    back_main = moved(away, 1, 0)
    away_side, away_corner, *inside = call(
        window_b_away_kernel, "window_b_away",
        [(quarter, D)] * 2 + [(cells, D)] * 3 + [bias_shape], [SMEM] + [VMEM] * 12,
        [wide], flops // 2 + each * 3 * quarter,
        pole_band, valid, far_side, far_corner, near_end, *near, *weights[0],
    )
    back_side = moved(away_side, 1, 0)
    back_corner = moved(away_corner, 1, 1)
    home_side, home_end = call(
        window_b_home_kernel, "window_b_home", [(quarter, D)] * 2, [VMEM] * 10,
        [wide], flops // 2,
        atmosphere, near_end, *inside, weights[0][0], *weights[0][2:],
    )
    back_end = moved(home_end, 0, 1)
    pair = (2, cells, D)
    inside = call(
        second_early_kernel, "second_early",
        [pair] * 3 + [jax.ShapeDtypeStruct((2, cells, cells), F32)],
        [VMEM] * 4 + [SMEM] + [VMEM] * 3, [], each * 6 * quarter,
        home, home_side, back_end, back_main, pole_band, valid, *weights[1][:2],
    )
    return call(
        second_kernel, "second", [(height, breadth, D)], [VMEM] * 15,
        [pltpu.VMEM(pair, BF16)] * 3 + [pltpu.VMEM((2 * cells, D), BF16)],
        2 * flops + each * 2 * quarter,
        home, home_side, back_end, back_main, back_side, back_corner, *inside, *weights[1],
    )[0]


def solution(mesh):
    in_specs = (
        P(("groups", "lat"), "lon", None),
        P(("groups", "lat")),
        P(("groups", "lat"), "lon"),
        P(),
        P(),
        P(),
        P(),
        P(),
    )
    out_specs = P(("groups", "lat"), "lon", None)
    return jax.shard_map(
        on_device, mesh=mesh, in_specs=in_specs, out_specs=out_specs, check_vma=False
    )
```

```python
import functools
import math

import jax
import jax.numpy as jnp
from jax import lax
from jax.experimental import pallas as pl
from jax.experimental.pallas import tpu as pltpu
from jax.sharding import PartitionSpec as P

D = 512
H = 8
WH = 32
WW = 16
HD = 64
SH = 16
SW = 8

norm_eps = 1e-05

F32 = jnp.float32
BF16 = jnp.bfloat16
CLASSES = 128
META = 16
QSCALE = math.log2(math.e) / math.sqrt(HD)
TRANSPOSED_RIGHT = (((1,), (1,)), ((), ()))
TRANSPOSED_LEFT = (((0,), (0,)), ((), ()))
VMEM = pl.BlockSpec(memory_space=pltpu.VMEM)
SMEM = pl.BlockSpec(memory_space=pltpu.SMEM)
HBM = pl.BlockSpec(memory_space=pltpu.HBM)


def product(left, right):
    return jnp.dot(left, right, preferred_element_type=F32)


def normalize(field, gains):
    average = jnp.mean(field, -1, keepdims=True)
    centred = field - average
    spread = jnp.mean(centred * centred, -1, keepdims=True)
    return (centred * lax.rsqrt(spread + norm_eps) * gains).astype(BF16)


def gelu(value):
    scale = math.sqrt(2.0 / math.pi)
    bent = jnp.tanh(value * (scale + (scale * 0.044715) * (value * value)))
    half = 0.5 * value
    return half + half * bent


def half_columns(block, start):
    part = block.astype(F32)[:, start : start + SW]
    return part.reshape(block.shape[0] * SW, D)


def mask_lanes(valid, low, start, lanes):
    columns, height = valid.shape
    row = lax.broadcasted_iota(jnp.int32, (height, lanes), 0)
    cell = lax.broadcasted_iota(jnp.int32, (height, lanes), 1)
    pick = (row == low + lax.div(cell, SW)).astype(F32).astype(BF16)
    spread = product(valid[...].astype(F32).astype(BF16), pick)
    column = lax.broadcasted_iota(jnp.int32, (columns, lanes), 0)
    own = start + lax.rem(lax.broadcasted_iota(jnp.int32, (columns, lanes), 1), SW)
    return jnp.sum(jnp.where(column == own, spread, 0.0), 0, keepdims=True)


def band_lanes(bands, start, rows, lanes):
    own = lax.div(lax.broadcasted_iota(jnp.int32, (1, lanes), 1), SW)
    found = jnp.zeros((1, lanes), jnp.int32)
    for row in range(rows):
        found = jnp.where(own == row, bands[start + row], found)
    return found.astype(F32)


def meta_rows(masks, bands):
    row = lax.broadcasted_iota(jnp.int32, (META, masks.shape[1]), 0)
    return jnp.where(row == 0, masks, jnp.where(row == 1, bands, 0.0)).astype(BF16)


def meta_of(ref, cells):
    tail = ref[pl.ds(cells, META), :].astype(F32)
    return tail[0:1, :cells], tail[1:2, :cells]


def in_turn(count, stages):
    state = [None] * count
    for step in range(count + len(stages) - 1):
        for index, stage in enumerate(stages):
            piece = step - index
            if 0 <= piece < count:
                state[piece] = stage(piece, state[piece])


def project(field, gain, attend_in, at, query, key, value):
    rows = pl.ds(at, field.shape[0])
    normed = normalize(field, gain)
    query[rows, :] = (product(normed, attend_in[:, :D]) * QSCALE).astype(BF16)
    key[rows, :] = product(normed, attend_in[:, D : 2 * D]).astype(BF16)
    value[rows, :] = product(normed, attend_in[:, 2 * D :]).astype(BF16)


def set_bias(bias, bands, masks):
    cells = bands.shape[1]
    classes = lax.broadcasted_iota(jnp.int32, (CLASSES, cells), 0).astype(F32)
    one_hot = (classes == bands).astype(F32).astype(BF16)
    same = lax.dot_general(one_hot, one_hot, TRANSPOSED_LEFT, preferred_element_type=F32)
    asking = lax.broadcasted_iota(jnp.int32, (cells, cells), 0)
    asked = lax.broadcasted_iota(jnp.int32, (cells, cells), 1)
    allowed = (same > 0.5) & ((masks > 0.5) | (asking == asked))
    bias[...] = jnp.where(allowed, 0.0, -1e30)


def attend(query, key, value, bias, context, low, count):
    first = lax.broadcasted_iota(jnp.int32, (1, 2 * HD), 1) < HD
    rows = pl.ds(low, count)
    sums = {}

    def lanes(unit):
        return slice(2 * HD * (unit // 2), 2 * HD * (unit // 2 + 1))

    def own(unit, inside, outside):
        return jnp.where(first, inside, outside) if unit % 2 == 0 else jnp.where(first, outside, inside)

    def score(unit, _):
        queries = query[rows, lanes(unit)]
        queries = own(unit, queries, jnp.zeros_like(queries))
        scores = lax.dot_general(
            queries, key[:, lanes(unit)], TRANSPOSED_RIGHT, preferred_element_type=F32
        )
        return scores + bias[rows, :]

    def weigh(unit, scores):
        return jnp.exp2(scores - jnp.max(scores, -1, keepdims=True)).astype(BF16)

    def gather(unit, weights):
        values = value[:, lanes(unit)]
        sums[unit] = product(weights, own(unit, values, jnp.ones_like(values)))
        if unit % 2 == 1:
            even, odd = sums.pop(unit - 1), sums.pop(unit)
            above = jnp.where(first, even, odd)
            below = pltpu.roll(jnp.where(first, odd, even), HD, 1)
            context[rows, lanes(unit)] = (above / below).astype(BF16)

    in_turn(H, (score, weigh, gather))


def finish(fields, context, low, piece, attend_out, gain, expand, contract, write):
    def start(index, _):
        rows = pl.ds(low + index * piece, piece)
        added = fields[index] + product(context[rows, :], attend_out[...])
        resid = added.astype(BF16).astype(F32)
        return resid, normalize(resid, gain)

    def widen(index, state):
        return state[0], product(state[1], expand[...])

    def bend(index, state):
        return state[0], gelu(state[1]).astype(BF16)

    def end(index, state):
        write(index, state[0] + product(state[1], contract[...]))

    in_turn(len(fields), (start, widen, bend, end))


def pack_main_kernel(block_hbm, valid_hbm, main, block, valid, sems):
    height = block_hbm.shape[0]
    rows = height - 2 * SH
    copies = (
        pltpu.make_async_copy(valid_hbm, valid, sems.at[0]),
        pltpu.make_async_copy(block_hbm.at[pl.ds(SH, rows)], block, sems.at[1]),
    )
    for copy in copies:
        copy.start()
    copies[0].wait()
    masks = mask_lanes(valid, SH, 0, D)
    main[pl.ds(rows * SW, META), :] = meta_rows(masks, jnp.zeros_like(masks))
    copies[1].wait()
    main[pl.ds(0, rows * SW), :] = half_columns(block[...], 0).astype(BF16)


def early_kernel(
    block, bands, valid, main, gains, attend_in,
    side, corner, row_end, query, key, value,
):
    gains, attend_in = (ref.at[0] for ref in (gains, attend_in))
    height = block.shape[0]
    rows = height - 2 * SH
    places = ((side, height - SH, 0), (corner, 0, 0), (row_end, 0, SW))
    for out, low, column in places:
        cells = SH * SW
        out[pl.ds(0, cells), :] = half_columns(block[low : low + SH], column).astype(BF16)
        masks = mask_lanes(valid, low, column, D)
        out[pl.ds(cells, META), :] = meta_rows(masks, band_lanes(bands, low, SH, D))
    local = half_columns(block[SH:], SW)
    project(local, gains[0:1], attend_in, 0, query, key, value)


def window_a_kernel(
    block, bands, valid, taken, near_query, near_key, near_value,
    gains, attend_in, attend_out, expand, contract,
    away, home, query, key, value, bias, context,
):
    gains, attend_in, attend_out, expand, contract = (ref.at[0] for ref in (gains, attend_in, attend_out, expand, contract))
    height = block.shape[0]
    rows = height - 2 * SH
    cells = rows * SW
    for near, whole in ((near_query, query), (near_key, key), (near_value, value)):
        whole[pl.ds(0, cells), :] = near[pl.ds(0, cells), :]
    local = half_columns(block[SH : SH + rows], SW)
    remote = taken[pl.ds(0, cells), :].astype(F32)
    project(remote, gains[0:1], attend_in, cells, query, key, value)
    row_bands = band_lanes(bands, SH, rows, cells)
    masks, _ = meta_of(taken, cells)
    set_bias(
        bias,
        jnp.concatenate([row_bands, row_bands], 1),
        jnp.concatenate([mask_lanes(valid, SH, SW, cells), masks], 1),
    )
    attend(query, key, value, bias, context, 0, 2 * cells)

    def write(index, out):
        (home, away)[index][...] = out.astype(BF16)

    finish([local, remote], context, 0, cells, attend_out, gains[1:2], expand, contract, write)


def window_b_away_kernel(
    bands, valid, taken_side, taken_corner, taken_end, near_query, near_key, near_value,
    gains, attend_in, attend_out, expand, contract,
    away_side, away_corner, query, key, value, bias, context,
):
    gains, attend_in, attend_out, expand, contract = (ref.at[0] for ref in (gains, attend_in, attend_out, expand, contract))
    height = bands.shape[0]
    cells = SH * SW
    for near, whole in ((near_query, query), (near_key, key), (near_value, value)):
        whole[pl.ds(0, cells), :] = near[pl.ds(near.shape[0] - cells, cells), :]
    fields = []
    bands_here = [band_lanes(bands, height - SH, SH, cells)]
    masks_here = [mask_lanes(valid, height - SH, SW, cells)]
    for taken in (taken_end, taken_side, taken_corner):
        fields.append(taken[pl.ds(0, cells), :].astype(F32))
        masks, row_bands = meta_of(taken, cells)
        masks_here.append(masks)
        bands_here.append(row_bands)
    project(jnp.concatenate(fields, 0), gains[0:1], attend_in, cells, query, key, value)
    set_bias(bias, jnp.concatenate(bands_here, 1), jnp.concatenate(masks_here, 1))
    attend(query, key, value, bias, context, 2 * cells, 2 * cells)

    def write(index, out):
        (away_side, away_corner)[index][...] = out.astype(BF16)

    finish(fields[1:], context, 2 * cells, cells, attend_out, gains[1:2], expand, contract, write)


def window_b_home_kernel(
    block, taken_end, query, key, value, bias, gains, attend_out, expand, contract,
    home_side, home_end, context,
):
    gains, attend_out, expand, contract = (ref.at[0] for ref in (gains, attend_out, expand, contract))
    height = block.shape[0]
    cells = SH * SW
    attend(query, key, value, bias, context, 0, 2 * cells)
    fields = [half_columns(block[height - SH :], SW), taken_end[pl.ds(0, cells), :].astype(F32)]

    def write(index, out):
        (home_side, home_end)[index][...] = out.astype(BF16)

    finish(fields, context, 0, cells, attend_out, gains[1:2], expand, contract, write)


def second_early_kernel(
    home, home_side, near_end, far, bands, valid, gains, attend_in,
    query, key, value, bias,
):
    gains, attend_in = (ref.at[1] for ref in (gains, attend_in))
    part = SH * SW
    low, high = slice(0, part), slice(part, 2 * part)
    windows = ((near_end[...], home[low], far[low]), (home[high], home_side[...], far[high]))
    for index, parts in enumerate(windows):
        field = jnp.concatenate([piece.astype(F32) for piece in parts], 0)
        project(field, gains[0:1], attend_in, 0, query.at[index], key.at[index], value.at[index])
        row = index * WH
        row_bands = band_lanes(bands, row, WH, 2 * part)
        near_masks = mask_lanes(valid, row, SW, 2 * part)
        far_masks = mask_lanes(valid, row, 0, 2 * part)
        far_bands = row_bands
        if index == 0:
            far_bands = jnp.concatenate([row_bands[:, part:], row_bands[:, :part]], 1)
            far_masks = jnp.concatenate([far_masks[:, part:], far_masks[:, :part]], 1)
        set_bias(
            bias.at[index],
            jnp.concatenate([row_bands, far_bands], 1),
            jnp.concatenate([near_masks, far_masks], 1),
        )


def second_kernel(
    home, home_side, near_end, far, far_side, far_corner,
    early_query, early_key, early_value, bias,
    gains, attend_in, attend_out, expand, contract,
    out_ref, query, key, value, context,
):
    gains, attend_in, attend_out, expand, contract = (ref.at[1] for ref in (gains, attend_in, attend_out, expand, contract))
    part = SH * SW
    low, high = slice(0, part), slice(part, 2 * part)
    windows = (
        (near_end[...], home[low], far[low], far_corner[...]),
        (home[high], home_side[...], far[high], far_side[...]),
    )
    windows = [[piece.astype(F32) for piece in parts] for parts in windows]
    late = 3 * part
    for early, whole in ((early_query, query), (early_key, key), (early_value, value)):
        whole[:, pl.ds(0, late), :] = early[:, pl.ds(0, late), :]
    for index, parts in enumerate(windows):
        project(parts[3], gains[0:1], attend_in, late, query.at[index], key.at[index], value.at[index])
    for index in range(len(windows)):
        attend(
            query.at[index], key.at[index], value.at[index], bias.at[index],
            context.at[pl.ds(4 * part * index, 4 * part)], 0, 4 * part,
        )
    fields = [jnp.concatenate(parts[at : at + 2], 0) for parts in windows for at in (0, 2)]
    near = {}

    def write(index, out):
        window = index // 2
        if index % 2 == 0:
            near[window] = out
            return
        if window == 0:
            out = jnp.concatenate([out[part:], out[:part]], 0)
        both = [piece.reshape(WH, SW, D) for piece in (out, near.pop(window))]
        out_ref[pl.ds(window * WH, WH)] = jnp.concatenate(both, 1).astype(BF16)

    finish(fields, context, 0, 2 * part, attend_out, gains[1:2], expand, contract, write)


def call(kernel, name, shapes, specs, scratch, flops, *operands, limit=40):
    flops = 1
    shapes = [shape if isinstance(shape, jax.ShapeDtypeStruct) else jax.ShapeDtypeStruct(shape, BF16)
              for shape in shapes]
    return pl.pallas_call(
        kernel,
        out_shape=shapes,
        in_specs=specs,
        out_specs=[VMEM] * len(shapes),
        scratch_shapes=scratch,
        compiler_params=pltpu.CompilerParams(vmem_limit_bytes=limit * 2**20),
        cost_estimate=pl.CostEstimate(flops=flops, bytes_accessed=flops, transcendentals=0),
        name=name,
    )(*operands)


def on_device(
    atmosphere, pole_band, key_valid, norm_gains, attend_in, attend_out, expand, contract
):
    height, breadth = atmosphere.shape[0], atmosphere.shape[1]
    assert height == 2 * WH and breadth == WW
    lons, lats = lax.axis_size("lon"), lax.axis_size("lat")

    def moved(value, lon_step, lat_step):
        pairs = [
            (lon * lats + lat, (lon + lon_step) % lons * lats + (lat + lat_step) % lats)
            for lon in range(lons)
            for lat in range(lats)
        ]
        return lax.ppermute(value, ("lon", "lat"), pairs)

    cells = WH * WW
    half, quarter = cells // 2, cells // 4
    wide = pltpu.VMEM((cells, D), BF16)
    bias_shape = jax.ShapeDtypeStruct((cells, cells), F32)
    bias_scratch = pltpu.VMEM((cells, cells), F32)
    hidden = expand.shape[-1]
    each = 2 * D * 3 * D
    flops = cells * 2 * D * (D + 2 * hidden) + 4 * cells * cells * D

    valid = key_valid.T
    main = call(
        pack_main_kernel, "pack_main", [(half + META, D)], [HBM] * 2,
        [pltpu.VMEM((WH, breadth, D), BF16), pltpu.VMEM(valid.shape, valid.dtype),
         pltpu.SemaphoreType.DMA((2,))],
        10**6, atmosphere, valid, limit=62,
    )[0]
    far_main = moved(main, -1, 0)

    weights = (norm_gains, attend_in, attend_out, expand, contract)
    side, corner, row_end, *near = call(
        early_kernel, "early", [(quarter + META, D)] * 3 + [(half + quarter, D)] * 3,
        [VMEM, SMEM] + [VMEM] * 4, [], each * (half + quarter),
        atmosphere, pole_band, valid, main, *weights[:2],
    )
    far_side = moved(side, -1, 0)
    far_corner = moved(corner, -1, -1)
    near_end = moved(row_end, 0, -1)

    away, home = call(
        window_a_kernel, "window_a", [(half, D)] * 2, [VMEM, SMEM] + [VMEM] * 10,
        [wide] * 3 + [bias_scratch, wide], flops + each * half,
        atmosphere, pole_band, valid, far_main, *near, *weights,
    )
    back_main = moved(away, 1, 0)
    away_side, away_corner, *inside = call(
        window_b_away_kernel, "window_b_away",
        [(quarter, D)] * 2 + [(cells, D)] * 3 + [bias_shape], [SMEM] + [VMEM] * 12,
        [wide], flops // 2 + each * 3 * quarter,
        pole_band, valid, far_side, far_corner, near_end, *near, *weights,
    )
    back_side = moved(away_side, 1, 0)
    back_corner = moved(away_corner, 1, 1)
    home_side, home_end = call(
        window_b_home_kernel, "window_b_home", [(quarter, D)] * 2, [VMEM] * 10,
        [wide], flops // 2,
        atmosphere, near_end, *inside, weights[0], *weights[2:],
    )
    back_end = moved(home_end, 0, 1)
    pair = (2, cells, D)
    inside = call(
        second_early_kernel, "second_early",
        [pair] * 3 + [jax.ShapeDtypeStruct((2, cells, cells), F32)],
        [VMEM] * 4 + [SMEM] + [VMEM] * 3, [], each * 6 * quarter,
        home, home_side, back_end, back_main, pole_band, valid, *weights[:2],
    )
    return call(
        second_kernel, "second", [(height, breadth, D)], [VMEM] * 15,
        [pltpu.VMEM(pair, BF16)] * 3 + [pltpu.VMEM((2 * cells, D), BF16)],
        2 * flops + each * 2 * quarter,
        home, home_side, back_end, back_main, back_side, back_corner, *inside, *weights,
    )[0]


def solution(mesh):
    in_specs = (
        P(("groups", "lat"), "lon", None),
        P(("groups", "lat")),
        P(("groups", "lat"), "lon"),
        P(),
        P(),
        P(),
        P(),
        P(),
    )
    out_specs = P(("groups", "lat"), "lon", None)
    return jax.shard_map(
        on_device, mesh=mesh, in_specs=in_specs, out_specs=out_specs, check_vma=False
    )
```

```python
import functools
import math

import jax
import jax.numpy as jnp
from jax import lax
from jax.experimental import pallas as pl
from jax.experimental.pallas import tpu as pltpu
from jax.sharding import PartitionSpec as P

D = 512
H = 8
WH = 32
WW = 16
HD = 64
SH = 16
SW = 8

norm_eps = 1e-05

F32 = jnp.float32
BF16 = jnp.bfloat16
CLASSES = 128
META = 16
QSCALE = math.log2(math.e) / math.sqrt(HD)
TRANSPOSED_RIGHT = (((1,), (1,)), ((), ()))
TRANSPOSED_LEFT = (((0,), (0,)), ((), ()))
VMEM = pl.BlockSpec(memory_space=pltpu.VMEM)
SMEM = pl.BlockSpec(memory_space=pltpu.SMEM)
HBM = pl.BlockSpec(memory_space=pltpu.HBM)


def product(left, right):
    return jnp.dot(left, right, preferred_element_type=F32)


def normalize(field, gains):
    average = jnp.mean(field, -1, keepdims=True)
    centred = field - average
    spread = jnp.mean(centred * centred, -1, keepdims=True)
    return (centred * lax.rsqrt(spread + norm_eps) * gains).astype(BF16)


def gelu(value):
    scale = math.sqrt(2.0 / math.pi)
    bent = jnp.tanh(value * (scale + (scale * 0.044715) * (value * value)))
    half = 0.5 * value
    return half + half * bent


def half_columns(block, start):
    part = block.astype(F32)[:, start : start + SW]
    return part.reshape(block.shape[0] * SW, D)


def mask_lanes(valid, low, start, lanes):
    columns, height = valid.shape
    row = lax.broadcasted_iota(jnp.int32, (height, lanes), 0)
    cell = lax.broadcasted_iota(jnp.int32, (height, lanes), 1)
    pick = (row == low + lax.div(cell, SW)).astype(F32).astype(BF16)
    spread = product(valid[...].astype(F32).astype(BF16), pick)
    column = lax.broadcasted_iota(jnp.int32, (columns, lanes), 0)
    own = start + lax.rem(lax.broadcasted_iota(jnp.int32, (columns, lanes), 1), SW)
    return jnp.sum(jnp.where(column == own, spread, 0.0), 0, keepdims=True)


def band_lanes(bands, start, rows, lanes):
    own = lax.div(lax.broadcasted_iota(jnp.int32, (1, lanes), 1), SW)
    found = jnp.zeros((1, lanes), jnp.int32)
    for row in range(rows):
        found = jnp.where(own == row, bands[start + row], found)
    return found.astype(F32)


def meta_rows(masks, bands):
    row = lax.broadcasted_iota(jnp.int32, (META, masks.shape[1]), 0)
    return jnp.where(row == 0, masks, jnp.where(row == 1, bands, 0.0)).astype(BF16)


def meta_of(ref, cells):
    tail = ref[pl.ds(cells, META), :].astype(F32)
    return tail[0:1, :cells], tail[1:2, :cells]


def in_turn(count, stages):
    state = [None] * count
    for step in range(count + len(stages) - 1):
        for index, stage in enumerate(stages):
            piece = step - index
            if 0 <= piece < count:
                state[piece] = stage(piece, state[piece])


def project(field, gain, attend_in, at, query, key, value):
    rows = pl.ds(at, field.shape[0])
    normed = normalize(field, gain)
    query[rows, :] = (product(normed, attend_in[:, :D]) * QSCALE).astype(BF16)
    key[rows, :] = product(normed, attend_in[:, D : 2 * D]).astype(BF16)
    value[rows, :] = product(normed, attend_in[:, 2 * D :]).astype(BF16)


def set_bias(bias, bands, masks):
    cells = bands.shape[1]
    classes = lax.broadcasted_iota(jnp.int32, (CLASSES, cells), 0).astype(F32)
    one_hot = (classes == bands).astype(F32).astype(BF16)
    same = lax.dot_general(one_hot, one_hot, TRANSPOSED_LEFT, preferred_element_type=F32)
    asking = lax.broadcasted_iota(jnp.int32, (cells, cells), 0)
    asked = lax.broadcasted_iota(jnp.int32, (cells, cells), 1)
    allowed = (same > 0.5) & ((masks > 0.5) | (asking == asked))
    bias[...] = jnp.where(allowed, 0.0, -1e30)


def attend(query, key, value, bias, context, low, count):
    first = lax.broadcasted_iota(jnp.int32, (1, 2 * HD), 1) < HD
    rows = pl.ds(low, count)
    sums = {}

    def lanes(unit):
        return slice(2 * HD * (unit // 2), 2 * HD * (unit // 2 + 1))

    def own(unit, inside, outside):
        return jnp.where(first, inside, outside) if unit % 2 == 0 else jnp.where(first, outside, inside)

    def score(unit, _):
        queries = query[rows, lanes(unit)]
        queries = own(unit, queries, jnp.zeros_like(queries))
        scores = lax.dot_general(
            queries, key[:, lanes(unit)], TRANSPOSED_RIGHT, preferred_element_type=F32
        )
        return scores + bias[rows, :]

    def weigh(unit, scores):
        return jnp.exp2(scores - jnp.max(scores, -1, keepdims=True)).astype(BF16)

    def gather(unit, weights):
        values = value[:, lanes(unit)]
        sums[unit] = product(weights, own(unit, values, jnp.ones_like(values)))
        if unit % 2 == 1:
            even, odd = sums.pop(unit - 1), sums.pop(unit)
            above = jnp.where(first, even, odd)
            below = pltpu.roll(jnp.where(first, odd, even), HD, 1)
            context[rows, lanes(unit)] = (above / below).astype(BF16)

    in_turn(H, (score, weigh, gather))


def finish(fields, context, lows, attend_out, gain, expand, contract, write):
    def start(index, _):
        rows = pl.ds(lows[index], fields[index].shape[0])
        added = fields[index] + product(context[rows, :], attend_out[...])
        resid = added.astype(BF16).astype(F32)
        return resid, normalize(resid, gain)

    def widen(index, state):
        return state[0], product(state[1], expand[...])

    def bend(index, state):
        return state[0], gelu(state[1]).astype(BF16)

    def end(index, state):
        write(index, state[0] + product(state[1], contract[...]))

    in_turn(len(fields), (start, widen, bend, end))


def pack_main_kernel(block_hbm, valid_hbm, main, token, block, valid, sems):
    height = block_hbm.shape[0]
    rows = height - 2 * SH
    copies = (
        pltpu.make_async_copy(valid_hbm, valid, sems.at[0]),
        pltpu.make_async_copy(block_hbm.at[pl.ds(SH, rows)], block, sems.at[1]),
    )
    for copy in copies:
        copy.start()
    token[...] = jnp.zeros_like(token)
    copies[0].wait()
    masks = mask_lanes(valid, SH, 0, D)
    main[pl.ds(rows * SW, META), :] = meta_rows(masks, jnp.zeros_like(masks))
    copies[1].wait()
    main[pl.ds(0, rows * SW), :] = half_columns(block[...], 0).astype(BF16)


def early_kernel(
    block, bands, valid, token, gains, attend_in,
    side, corner, row_end, cells_here, query, key, value, notes,
):
    height = block.shape[0]
    part = SH * SW
    for out, low, column in ((side, height - SH, 0), (corner, 0, 0), (row_end, 0, SW)):
        out[pl.ds(0, part), :] = half_columns(block[low : low + SH], column).astype(BF16)
        masks = mask_lanes(valid, low, column, D)
        out[pl.ds(part, META), :] = meta_rows(masks, band_lanes(bands, low, SH, D))
    local = half_columns(block[SH:], SW)
    cells_here[...] = local.astype(BF16)
    window_notes = [
        (band_lanes(bands, SH, height - SH, D), mask_lanes(valid, SH, SW, D)),
    ]
    for row in range(0, height, WH):
        row_bands = band_lanes(bands, row, WH, 2 * part)
        window_notes.append((
            jnp.concatenate([row_bands, row_bands], 1),
            jnp.concatenate(
                [mask_lanes(valid, row, SW, 2 * part), mask_lanes(valid, row, 0, 2 * part)], 1
            ),
        ))
    for index, pair in enumerate(window_notes):
        for offset, lanes in enumerate(pair):
            notes[pl.ds(2 * index + offset, 1), :] = lanes
    project(local, gains[0:1], attend_in, 0, query, key, value)


def window_a_kernel(
    cells_here, notes, taken, near_query, near_key, near_value,
    gains, attend_in, attend_out, expand, contract,
    away, home, query, key, value, bias, context,
):
    cells = away.shape[0]
    for near, whole in ((near_query, query), (near_key, key), (near_value, value)):
        whole[pl.ds(0, cells), :] = near[pl.ds(0, cells), :]
    local = cells_here[pl.ds(0, cells), :].astype(F32)
    remote = taken[pl.ds(0, cells), :].astype(F32)
    project(remote, gains[0:1], attend_in, cells, query, key, value)
    row_bands = notes[0:1, :cells]
    masks, _ = meta_of(taken, cells)
    set_bias(
        bias,
        jnp.concatenate([row_bands, row_bands], 1),
        jnp.concatenate([notes[1:2, :cells], masks], 1),
    )
    attend(query, key, value, bias, context, 0, 2 * cells)

    def write(index, out):
        (home, away)[index][...] = out.astype(BF16)

    finish([local, remote], context, (0, cells), attend_out, gains[1:2], expand, contract, write)


def window_b_away_kernel(
    window_a_first, notes, taken_side, taken_corner, taken_end, near_query, near_key, near_value,
    gains, attend_in, attend_out, expand, contract,
    away_side, away_corner, home_end, query, key, value, bias, context,
):
    cells = away_side.shape[0]
    skip = near_query.shape[0] - cells
    for near, whole in ((near_query, query), (near_key, key), (near_value, value)):
        whole[pl.ds(0, cells), :] = near[pl.ds(skip, cells), :]
    fields = []
    bands_here = [notes[0:1, skip : skip + cells]]
    masks_here = [notes[1:2, skip : skip + cells]]
    for taken in (taken_end, taken_side, taken_corner):
        fields.append(taken[pl.ds(0, cells), :].astype(F32))
        masks, row_bands = meta_of(taken, cells)
        masks_here.append(masks)
        bands_here.append(row_bands)
    bands_here[2] = bands_here[0]
    project(jnp.concatenate(fields, 0), gains[0:1], attend_in, cells, query, key, value)
    set_bias(bias, jnp.concatenate(bands_here, 1), jnp.concatenate(masks_here, 1))
    attend(query, key, value, bias, context, cells, 3 * cells)

    def write(index, out):
        out = out.astype(BF16)
        if index == 0:
            away_side[...], away_corner[...] = out[:cells], out[cells:]
        else:
            home_end[...] = out

    fields = [jnp.concatenate(fields[1:], 0), fields[0]]
    finish(fields, context, (2 * cells, cells), attend_out, gains[1:2], expand, contract, write)


def between_kernel(
    cells_here, query, key, value, bias, gains, attend_out, expand, contract,
    home, notes, next_gains, next_attend_in,
    home_side, next_query, next_key, next_value, next_bias, context,
):
    part = home_side.shape[0]
    attend(query, key, value, bias, context, 0, part)
    near = cells_here[pl.ds(cells_here.shape[0] - part, part), :]
    kept = []

    def write(index, out):
        home_side[...] = out.astype(BF16)
        kept.append(out.astype(BF16).astype(F32))

    finish([near.astype(F32)], context, (0,), attend_out, gains[1:2], expand, contract, write)
    for index in range(2):
        set_bias(next_bias.at[index], notes[2 * index + 2 : 2 * index + 3],
                 notes[2 * index + 3 : 2 * index + 4])
    pieces = ((0, part, home[:part].astype(F32)),
              (1, 0, jnp.concatenate([home[part:].astype(F32), kept[0]], 0)))
    for index, at, field in pieces:
        project(field, next_gains[0:1], next_attend_in, at,
                next_query.at[index], next_key.at[index], next_value.at[index])


def second_kernel(
    home, home_side, far, far_side, far_corner, near_end,
    early_query, early_key, early_value, bias,
    gains, attend_in, attend_out, expand, contract,
    out_ref, query, key, value, context,
):
    part = SH * SW
    low, high = slice(0, part), slice(part, 2 * part)
    windows = (
        (near_end[...], home[low], far_corner[...], far[low]),
        (home[high], home_side[...], far[high], far_side[...]),
    )
    windows = [[piece.astype(F32) for piece in parts] for parts in windows]
    pieces = ((0, 0, windows[0][0]), (0, 2 * part, jnp.concatenate(windows[0][2:], 0)),
              (1, 2 * part, jnp.concatenate(windows[1][2:], 0)))
    for index, at, field in pieces:
        project(field, gains[0:1], attend_in, at, query.at[index], key.at[index], value.at[index])
    for index in range(len(windows)):
        attend(
            query.at[index], key.at[index], value.at[index], bias.at[index],
            context.at[pl.ds(4 * part * index, 4 * part)], 0, 4 * part,
        )
    fields = [jnp.concatenate(parts[at : at + 2], 0) for parts in windows for at in (0, 2)]
    near = {}

    def write(index, out):
        window = index // 2
        if index % 2 == 0:
            near[window] = out
            return
        both = [piece.reshape(WH, SW, D) for piece in (out, near.pop(window))]
        out_ref[pl.ds(window * WH, WH)] = jnp.concatenate(both, 1).astype(BF16)

    lows = [2 * part * at for at in range(len(fields))]
    finish(fields, context, lows, attend_out, gains[1:2], expand, contract, write)


def call(kernel, name, shapes, specs, scratch, flops, *operands, limit=40, aliases=()):
    size = sum(operand.size * operand.dtype.itemsize for operand in operands)
    shapes = [shape if isinstance(shape, jax.ShapeDtypeStruct) else jax.ShapeDtypeStruct(shape, BF16)
              for shape in shapes]
    return pl.pallas_call(
        kernel,
        out_shape=shapes,
        in_specs=specs,
        out_specs=[VMEM] * len(shapes),
        scratch_shapes=scratch,
        compiler_params=pltpu.CompilerParams(vmem_limit_bytes=limit * 2**20),
        cost_estimate=pl.CostEstimate(flops=flops, bytes_accessed=size, transcendentals=0),
        input_output_aliases=dict(aliases),
        name=name,
    )(*operands)


def on_device(
    atmosphere, pole_band, key_valid, norm_gains, attend_in, attend_out, expand, contract
):
    height, breadth = atmosphere.shape[0], atmosphere.shape[1]
    assert height == 2 * WH and breadth == WW
    lons, lats = lax.axis_size("lon"), lax.axis_size("lat")

    def moved(value, lon_step, lat_step):
        pairs = [
            (lon * lats + lat, (lon + lon_step) % lons * lats + (lat + lat_step) % lats)
            for lon in range(lons)
            for lat in range(lats)
        ]
        return lax.ppermute(value, ("lon", "lat"), pairs)

    cells = WH * WW
    half, quarter = cells // 2, cells // 4
    wide = pltpu.VMEM((cells, D), BF16)
    bias_shape = jax.ShapeDtypeStruct((cells, cells), F32)
    bias_scratch = pltpu.VMEM((cells, cells), F32)
    hidden = expand.shape[-1]
    each = 2 * D * 3 * D
    flops = cells * 2 * D * (D + 2 * hidden) + 4 * cells * cells * D

    valid = key_valid.T
    valid_scratch = pltpu.VMEM(valid.shape, valid.dtype)
    main, token = call(
        pack_main_kernel, "pack_main", [(half + META, D), (META, 2 * HD)], [HBM] * 2,
        [pltpu.VMEM((WH, breadth, D), BF16), valid_scratch, pltpu.SemaphoreType.DMA((2,))],
        10**6, atmosphere, valid, limit=62,
    )
    far_main = moved(main, -1, 0)

    weights = [
        (norm_gains[k], attend_in[k], attend_out[k], expand[k], contract[k]) for k in range(2)
    ]
    side, corner, row_end, here, *near, notes = call(
        early_kernel, "early",
        [(quarter + META, D)] * 3 + [(half + quarter, D)] * 4
        + [jax.ShapeDtypeStruct((META, D), F32)],
        [VMEM, SMEM] + [VMEM] * 4, [], each * (half + quarter),
        atmosphere, pole_band, valid, token, *weights[0][:2],
    )
    far_side = moved(side, -1, 0)
    far_corner = moved(corner, -1, -1)
    near_end = moved(row_end, 0, -1)

    away, home = call(
        window_a_kernel, "window_a", [(half, D)] * 2, [VMEM] * 11,
        [wide] * 3 + [bias_scratch, wide], flops + each * half,
        here, notes, far_main, *near, *weights[0],
    )
    back_main = moved(away, 1, 0)
    away_side, away_corner, home_end, *inside = call(
        window_b_away_kernel, "window_b_away",
        [(quarter, D)] * 3 + [(cells, D)] * 3 + [bias_shape], [VMEM] * 13,
        [wide], 3 * flops // 4 + each * 3 * quarter,
        home, notes, far_side, far_corner, near_end, *near, *weights[0],
    )
    pair = (2, cells, D)
    home_side, *inside = call(
        between_kernel, "between",
        [(quarter, D)] + [pair] * 3 + [jax.ShapeDtypeStruct((2, cells, cells), F32)],
        [VMEM] * 13, [wide], flops // 4 + each * 3 * quarter,
        here, *inside, weights[0][0], *weights[0][2:],
        home, notes, *weights[1][:2],
    )
    back_side = moved(away_side, 1, 0)
    back_corner = moved(away_corner, 1, 1)
    back_end = moved(home_end, 0, 1)
    return call(
        second_kernel, "second", [(height, breadth, D)] + [pair] * 3, [VMEM] * 15,
        [pltpu.VMEM((2 * cells, D), BF16)],
        2 * flops + each * 5 * quarter,
        home, home_side, back_main, back_side, back_corner, back_end, *inside, *weights[1],
        aliases=((6, 1), (7, 2), (8, 3)),
    )[0]


def solution(mesh):
    in_specs = (
        P(("groups", "lat"), "lon", None),
        P(("groups", "lat")),
        P(("groups", "lat"), "lon"),
        P(),
        P(),
        P(),
        P(),
        P(),
    )
    out_specs = P(("groups", "lat"), "lon", None)
    return jax.shard_map(
        on_device, mesh=mesh, in_specs=in_specs, out_specs=out_specs, check_vma=False
    )
```

```python
import functools
import math

import jax
import jax.numpy as jnp
from jax import lax
from jax.experimental import pallas as pl
from jax.experimental.pallas import tpu as pltpu
from jax.sharding import PartitionSpec as P

D = 512
H = 8
WH = 32
WW = 16
HD = 64
SH = 16
SW = 8

norm_eps = 1e-05

F32 = jnp.float32
BF16 = jnp.bfloat16
CLASSES = 128
META = 16
QSCALE = math.log2(math.e) / math.sqrt(HD)
TRANSPOSED_RIGHT = (((1,), (1,)), ((), ()))
TRANSPOSED_LEFT = (((0,), (0,)), ((), ()))
VMEM = pl.BlockSpec(memory_space=pltpu.VMEM)
SMEM = pl.BlockSpec(memory_space=pltpu.SMEM)
HBM = pl.BlockSpec(memory_space=pltpu.HBM)


def product(left, right):
    return jnp.dot(left, right, preferred_element_type=F32)


def normalize(field, gains):
    average = jnp.mean(field, -1, keepdims=True)
    centred = field - average
    spread = jnp.mean(centred * centred, -1, keepdims=True)
    return (centred * lax.rsqrt(spread + norm_eps) * gains).astype(BF16)


def gelu(value):
    scale = math.sqrt(2.0 / math.pi)
    bent = jnp.tanh(value * (scale + (scale * 0.044715) * (value * value)))
    half = 0.5 * value
    return half + half * bent


def half_columns(block, start):
    part = block.astype(F32)[:, start : start + SW]
    return part.reshape(block.shape[0] * SW, D)


def mask_lanes(valid, low, start, lanes):
    columns, height = valid.shape
    row = lax.broadcasted_iota(jnp.int32, (height, lanes), 0)
    cell = lax.broadcasted_iota(jnp.int32, (height, lanes), 1)
    pick = (row == low + lax.div(cell, SW)).astype(F32).astype(BF16)
    spread = product(valid[...].astype(F32).astype(BF16), pick)
    column = lax.broadcasted_iota(jnp.int32, (columns, lanes), 0)
    own = start + lax.rem(lax.broadcasted_iota(jnp.int32, (columns, lanes), 1), SW)
    return jnp.sum(jnp.where(column == own, spread, 0.0), 0, keepdims=True)


def band_lanes(bands, start, rows, lanes):
    own = lax.div(lax.broadcasted_iota(jnp.int32, (1, lanes), 1), SW)
    found = jnp.zeros((1, lanes), jnp.int32)
    for row in range(rows):
        found = jnp.where(own == row, bands[start + row], found)
    return found.astype(F32)


def meta_rows(masks, bands):
    row = lax.broadcasted_iota(jnp.int32, (META, masks.shape[1]), 0)
    return jnp.where(row == 0, masks, jnp.where(row == 1, bands, 0.0)).astype(BF16)


def meta_of(ref, cells):
    tail = ref[pl.ds(cells, META), :].astype(F32)
    return tail[0:1, :cells], tail[1:2, :cells]


def in_turn(count, stages):
    state = [None] * count
    for step in range(count + len(stages) - 1):
        for index, stage in enumerate(stages):
            piece = step - index
            if 0 <= piece < count:
                state[piece] = stage(piece, state[piece])


def project(field, gain, attend_in, at, query, key, value):
    rows = pl.ds(at, field.shape[0])
    normed = normalize(field, gain)
    query[rows, :] = (product(normed, attend_in[:, :D]) * QSCALE).astype(BF16)
    key[rows, :] = product(normed, attend_in[:, D : 2 * D]).astype(BF16)
    value[rows, :] = product(normed, attend_in[:, 2 * D :]).astype(BF16)


def set_bias(bias, bands, masks):
    cells = bands.shape[1]
    classes = lax.broadcasted_iota(jnp.int32, (CLASSES, cells), 0).astype(F32)
    one_hot = (classes == bands).astype(F32).astype(BF16)
    same = lax.dot_general(one_hot, one_hot, TRANSPOSED_LEFT, preferred_element_type=F32)
    asking = lax.broadcasted_iota(jnp.int32, (cells, cells), 0)
    asked = lax.broadcasted_iota(jnp.int32, (cells, cells), 1)
    allowed = (same > 0.5) & ((masks > 0.5) | (asking == asked))
    bias[...] = jnp.where(allowed, 0.0, -1e30)


def attend(query, key, value, bias, context, low, count):
    first = lax.broadcasted_iota(jnp.int32, (1, 2 * HD), 1) < HD
    rows = pl.ds(low, count)
    sums = {}

    def lanes(unit):
        return slice(2 * HD * (unit // 2), 2 * HD * (unit // 2 + 1))

    def own(unit, inside, outside):
        return jnp.where(first, inside, outside) if unit % 2 == 0 else jnp.where(first, outside, inside)

    def score(unit, _):
        queries = query[rows, lanes(unit)]
        queries = own(unit, queries, jnp.zeros_like(queries))
        scores = lax.dot_general(
            queries, key[:, lanes(unit)], TRANSPOSED_RIGHT, preferred_element_type=F32
        )
        return scores + bias[rows, :]

    def weigh(unit, scores):
        return jnp.exp2(scores - jnp.max(scores, -1, keepdims=True)).astype(BF16)

    def gather(unit, weights):
        values = value[:, lanes(unit)]
        sums[unit] = product(weights, own(unit, values, jnp.ones_like(values)))
        if unit % 2 == 1:
            even, odd = sums.pop(unit - 1), sums.pop(unit)
            above = jnp.where(first, even, odd)
            below = pltpu.roll(jnp.where(first, odd, even), HD, 1)
            context[rows, lanes(unit)] = (above / below).astype(BF16)

    in_turn(H, (score, weigh, gather))


def finish(fields, context, lows, attend_out, gain, expand, contract, write):
    def start(index, _):
        rows = pl.ds(lows[index], fields[index].shape[0])
        added = fields[index] + product(context[rows, :], attend_out[...])
        resid = added.astype(BF16).astype(F32)
        return resid, normalize(resid, gain)

    def widen(index, state):
        return state[0], product(state[1], expand[...])

    def bend(index, state):
        return state[0], gelu(state[1]).astype(BF16)

    def end(index, state):
        write(index, state[0] + product(state[1], contract[...]))

    in_turn(len(fields), (start, widen, bend, end))


def pack_main_kernel(block_hbm, valid_hbm, main, token, block, valid, sems):
    height = block_hbm.shape[0]
    rows = height - 2 * SH
    copies = (
        pltpu.make_async_copy(valid_hbm, valid, sems.at[0]),
        pltpu.make_async_copy(block_hbm.at[pl.ds(SH, rows)], block, sems.at[1]),
    )
    for copy in copies:
        copy.start()
    token[...] = jnp.zeros_like(token)
    copies[0].wait()
    masks = mask_lanes(valid, SH, 0, D)
    main[pl.ds(rows * SW, META), :] = meta_rows(masks, jnp.zeros_like(masks))
    copies[1].wait()
    main[pl.ds(0, rows * SW), :] = half_columns(block[...], 0).astype(BF16)


def early_kernel(
    block, bands, valid, token, gains, attend_in,
    side, corner, row_end, cells_here, query, key, value, notes,
):
    height = block.shape[0]
    part = SH * SW
    for out, low, column in ((side, height - SH, 0), (corner, 0, 0), (row_end, 0, SW)):
        out[pl.ds(0, part), :] = half_columns(block[low : low + SH], column).astype(BF16)
        masks = mask_lanes(valid, low, column, D)
        out[pl.ds(part, META), :] = meta_rows(masks, band_lanes(bands, low, SH, D))
    local = half_columns(block[SH:], SW)
    cells_here[...] = local.astype(BF16)
    window_notes = [
        (band_lanes(bands, SH, height - SH, D), mask_lanes(valid, SH, SW, D)),
    ]
    for row in range(0, height, WH):
        row_bands = band_lanes(bands, row, WH, 2 * part)
        window_notes.append((
            jnp.concatenate([row_bands, row_bands], 1),
            jnp.concatenate(
                [mask_lanes(valid, row, SW, 2 * part), mask_lanes(valid, row, 0, 2 * part)], 1
            ),
        ))
    for index, pair in enumerate(window_notes):
        for offset, lanes in enumerate(pair):
            notes[pl.ds(2 * index + offset, 1), :] = lanes
    project(local, gains[0, 0:1], attend_in, 0, query, key, value)


def window_a_kernel(
    cells_here, notes, taken, near_query, near_key, near_value,
    gains, attend_in, attend_out, expand, contract,
    away, home, query, key, value, bias, context,
):
    cells = away.shape[0]
    for near, whole in ((near_query, query), (near_key, key), (near_value, value)):
        whole[pl.ds(0, cells), :] = near[pl.ds(0, cells), :]
    local = cells_here[pl.ds(0, cells), :].astype(F32)
    remote = taken[pl.ds(0, cells), :].astype(F32)
    project(remote, gains[0, 0:1], attend_in, cells, query, key, value)
    row_bands = notes[0:1, :cells]
    masks, _ = meta_of(taken, cells)
    set_bias(
        bias,
        jnp.concatenate([row_bands, row_bands], 1),
        jnp.concatenate([notes[1:2, :cells], masks], 1),
    )
    attend(query, key, value, bias, context, 0, 2 * cells)

    def write(index, out):
        (home, away)[index][...] = out.astype(BF16)

    finish([local, remote], context, (0, cells), attend_out, gains[0, 1:2], expand, contract, write)


def window_b_away_kernel(
    window_a_first, notes, taken_side, taken_corner, taken_end, near_query, near_key, near_value,
    gains, attend_in, attend_out, expand, contract,
    away_side, away_corner, home_end, query, key, value, bias, context,
):
    cells = away_side.shape[0]
    skip = near_query.shape[0] - cells
    for near, whole in ((near_query, query), (near_key, key), (near_value, value)):
        whole[pl.ds(0, cells), :] = near[pl.ds(skip, cells), :]
    fields = []
    bands_here = [notes[0:1, skip : skip + cells]]
    masks_here = [notes[1:2, skip : skip + cells]]
    for taken in (taken_end, taken_side, taken_corner):
        fields.append(taken[pl.ds(0, cells), :].astype(F32))
        masks, row_bands = meta_of(taken, cells)
        masks_here.append(masks)
        bands_here.append(row_bands)
    bands_here[2] = bands_here[0]
    project(jnp.concatenate(fields, 0), gains[0, 0:1], attend_in, cells, query, key, value)
    set_bias(bias, jnp.concatenate(bands_here, 1), jnp.concatenate(masks_here, 1))
    attend(query, key, value, bias, context, cells, 3 * cells)

    def write(index, out):
        out = out.astype(BF16)
        if index == 0:
            away_side[...], away_corner[...] = out[:cells], out[cells:]
        else:
            home_end[...] = out

    fields = [jnp.concatenate(fields[1:], 0), fields[0]]
    finish(fields, context, (2 * cells, cells), attend_out, gains[0, 1:2], expand, contract, write)


def between_kernel(
    cells_here, query, key, value, bias, gains, attend_out, expand, contract,
    home, far, notes, next_gains, next_attend_in,
    home_side, next_query, next_key, next_value, next_bias, context,
):
    part = home_side.shape[0]
    attend(query, key, value, bias, context, 0, part)
    near = cells_here[pl.ds(cells_here.shape[0] - part, part), :]
    kept = []

    def write(index, out):
        home_side[...] = out.astype(BF16)
        kept.append(out.astype(BF16).astype(F32))

    finish([near.astype(F32)], context, (0,), attend_out, gains[0, 1:2], expand, contract, write)
    for index in range(2):
        set_bias(next_bias.at[index], notes[2 * index + 2 : 2 * index + 3],
                 notes[2 * index + 3 : 2 * index + 4])
    pieces = ((0, part, home[:part].astype(F32)),
              (0, 3 * part, far[:part].astype(F32)),
              (1, 0, jnp.concatenate([home[part:].astype(F32), kept[0], far[part:].astype(F32)], 0)))
    for index, at, field in pieces:
        project(field, next_gains[1, 0:1], next_attend_in.at[1], at,
                next_query.at[index], next_key.at[index], next_value.at[index])


def second_kernel(
    home, home_side, far, far_side, far_corner, near_end,
    early_query, early_key, early_value, bias,
    gains, attend_in, attend_out, expand, contract,
    out_hbm, query, key, value, context, out_ref, sems,
):
    part = SH * SW
    copies = []
    low, high = slice(0, part), slice(part, 2 * part)
    windows = (
        (near_end[...], home[low], far_corner[...], far[low]),
        (home[high], home_side[...], far[high], far_side[...]),
    )
    windows = [[piece.astype(F32) for piece in parts] for parts in windows]
    pieces = ((0, 0, windows[0][0]), (0, 2 * part, windows[0][2]), (1, 3 * part, windows[1][3]))
    for index, at, field in pieces:
        project(field, gains[1, 0:1], attend_in.at[1], at, query.at[index], key.at[index], value.at[index])
    for index in range(len(windows)):
        attend(
            query.at[index], key.at[index], value.at[index], bias.at[index],
            context.at[pl.ds(4 * part * index, 4 * part)], 0, 4 * part,
        )
    fields = [jnp.concatenate(parts[at : at + 2], 0) for parts in windows for at in (0, 2)]
    near = {}

    def write(index, out):
        window = index // 2
        if index % 2 == 0:
            near[window] = out
            return
        both = [piece.reshape(WH, SW, D) for piece in (out, near.pop(window))]
        rows = pl.ds(window * WH, WH)
        out_ref[rows] = jnp.concatenate(both, 1).astype(BF16)
        copies.append(pltpu.make_async_copy(out_ref.at[rows], out_hbm.at[rows], sems.at[window]))
        copies[-1].start()

    lows = [2 * part * at for at in range(len(fields))]
    finish(fields, context, lows, attend_out.at[1], gains[1, 1:2], expand.at[1], contract.at[1], write)
    for copy in copies:
        copy.wait()


def call(kernel, name, shapes, specs, scratch, flops, *operands, limit=40, aliases=(), outs=VMEM):
    size = sum(operand.size * operand.dtype.itemsize for operand in operands)
    shapes = [shape if isinstance(shape, jax.ShapeDtypeStruct) else jax.ShapeDtypeStruct(shape, BF16)
              for shape in shapes]
    return pl.pallas_call(
        kernel,
        out_shape=shapes,
        in_specs=specs,
        out_specs=[outs] + [VMEM] * (len(shapes) - 1),
        scratch_shapes=scratch,
        compiler_params=pltpu.CompilerParams(vmem_limit_bytes=limit * 2**20),
        cost_estimate=pl.CostEstimate(flops=flops, bytes_accessed=size, transcendentals=0),
        input_output_aliases=dict(aliases),
        name=name,
    )(*operands)


def on_device(
    atmosphere, pole_band, key_valid, norm_gains, attend_in, attend_out, expand, contract
):
    height, breadth = atmosphere.shape[0], atmosphere.shape[1]
    assert height == 2 * WH and breadth == WW
    lons, lats = lax.axis_size("lon"), lax.axis_size("lat")

    def moved(value, lon_step, lat_step):
        pairs = [
            (lon * lats + lat, (lon + lon_step) % lons * lats + (lat + lat_step) % lats)
            for lon in range(lons)
            for lat in range(lats)
        ]
        return lax.ppermute(value, ("lon", "lat"), pairs)

    cells = WH * WW
    half, quarter = cells // 2, cells // 4
    wide = pltpu.VMEM((cells, D), BF16)
    bias_shape = jax.ShapeDtypeStruct((cells, cells), F32)
    bias_scratch = pltpu.VMEM((cells, cells), F32)
    hidden = expand.shape[-1]
    each = 2 * D * 3 * D
    flops = cells * 2 * D * (D + 2 * hidden) + 4 * cells * cells * D

    valid = key_valid.T
    valid_scratch = pltpu.VMEM(valid.shape, valid.dtype)
    main, token = call(
        pack_main_kernel, "pack_main", [(half + META, D), (META, 2 * HD)], [HBM] * 2,
        [pltpu.VMEM((WH, breadth, D), BF16), valid_scratch, pltpu.SemaphoreType.DMA((2,))],
        10**6, atmosphere, valid, limit=62,
    )
    far_main = moved(main, -1, 0)

    weights = [
        (norm_gains, attend_in[0], attend_out[0], expand[0], contract[0]),
        (norm_gains, attend_in, attend_out, expand, contract),
    ]
    side, corner, row_end, here, *near, notes = call(
        early_kernel, "early",
        [(quarter + META, D)] * 3 + [(half + quarter, D)] * 4
        + [jax.ShapeDtypeStruct((META, D), F32)],
        [VMEM, SMEM] + [VMEM] * 4, [], each * (half + quarter),
        atmosphere, pole_band, valid, token, *weights[0][:2],
    )
    far_side = moved(side, -1, 0)
    far_corner = moved(corner, -1, -1)
    near_end = moved(row_end, 0, -1)

    away, home = call(
        window_a_kernel, "window_a", [(half, D)] * 2, [VMEM] * 11,
        [wide] * 3 + [bias_scratch, wide], flops + each * half,
        here, notes, far_main, *near, *weights[0],
    )
    back_main = moved(away, 1, 0)
    away_side, away_corner, home_end, *inside = call(
        window_b_away_kernel, "window_b_away",
        [(quarter, D)] * 3 + [(cells, D)] * 3 + [bias_shape], [VMEM] * 13,
        [wide], 3 * flops // 4 + each * 3 * quarter,
        home, notes, far_side, far_corner, near_end, *near, *weights[0],
    )
    pair = (2, cells, D)
    home_side, *inside = call(
        between_kernel, "between",
        [(quarter, D)] + [pair] * 3 + [jax.ShapeDtypeStruct((2, cells, cells), F32)],
        [VMEM] * 14, [wide], flops // 4 + each * 5 * quarter,
        here, *inside, weights[0][0], *weights[0][2:],
        home, back_main, notes, *weights[1][:2],
    )
    back_side = moved(away_side, 1, 0)
    back_corner = moved(away_corner, 1, 1)
    back_end = moved(home_end, 0, 1)
    return call(
        second_kernel, "second", [(height, breadth, D)] + [pair] * 3, [VMEM] * 15,
        [pltpu.VMEM((2 * cells, D), BF16), pltpu.VMEM(atmosphere.shape, BF16),
         pltpu.SemaphoreType.DMA((2,))],
        2 * flops + each * 5 * quarter,
        home, home_side, back_main, back_side, back_corner, back_end, *inside, *weights[1],
        aliases=((6, 1), (7, 2), (8, 3)), outs=HBM,
    )[0]


def solution(mesh):
    in_specs = (
        P(("groups", "lat"), "lon", None),
        P(("groups", "lat")),
        P(("groups", "lat"), "lon"),
        P(),
        P(),
        P(),
        P(),
        P(),
    )
    out_specs = P(("groups", "lat"), "lon", None)
    return jax.shard_map(
        on_device, mesh=mesh, in_specs=in_specs, out_specs=out_specs, check_vma=False
    )
```

```python
import functools
import math

import jax
import jax.numpy as jnp
from jax import lax
from jax.experimental import pallas as pl
from jax.experimental.pallas import tpu as pltpu
from jax.sharding import PartitionSpec as P

D = 512
H = 8
WH = 32
WW = 16
HD = 64
SH = 16
SW = 8

norm_eps = 1e-05

F32 = jnp.float32
BF16 = jnp.bfloat16
CLASSES = 128
META = 16
QSCALE = math.log2(math.e) / math.sqrt(HD)
TRANSPOSED_RIGHT = (((1,), (1,)), ((), ()))
TRANSPOSED_LEFT = (((0,), (0,)), ((), ()))
VMEM = pl.BlockSpec(memory_space=pltpu.VMEM)
SMEM = pl.BlockSpec(memory_space=pltpu.SMEM)
HBM = pl.BlockSpec(memory_space=pltpu.HBM)


def product(left, right):
    return jnp.dot(left, right, preferred_element_type=F32)


def normalize(field, gains):
    average = jnp.mean(field, -1, keepdims=True)
    centred = field - average
    spread = jnp.mean(centred * centred, -1, keepdims=True)
    return (centred * lax.rsqrt(spread + norm_eps) * gains).astype(BF16)


def gelu(value):
    scale = math.sqrt(2.0 / math.pi)
    bent = jnp.tanh(value * (scale + (scale * 0.044715) * (value * value)))
    half = 0.5 * value
    return half + half * bent


def half_columns(block, start):
    part = block.astype(F32)[:, start : start + SW]
    return part.reshape(block.shape[0] * SW, D)


def mask_lanes(valid, low, start, lanes):
    columns, height = valid.shape
    row = lax.broadcasted_iota(jnp.int32, (height, lanes), 0)
    cell = lax.broadcasted_iota(jnp.int32, (height, lanes), 1)
    pick = (row == low + lax.div(cell, SW)).astype(F32).astype(BF16)
    spread = product(valid[...].astype(F32).astype(BF16), pick)
    column = lax.broadcasted_iota(jnp.int32, (columns, lanes), 0)
    own = start + lax.rem(lax.broadcasted_iota(jnp.int32, (columns, lanes), 1), SW)
    return jnp.sum(jnp.where(column == own, spread, 0.0), 0, keepdims=True)


def band_lanes(bands, start, rows, lanes):
    own = lax.div(lax.broadcasted_iota(jnp.int32, (1, lanes), 1), SW)
    found = jnp.zeros((1, lanes), jnp.int32)
    for row in range(rows):
        found = jnp.where(own == row, bands[start + row], found)
    return found.astype(F32)


def meta_rows(masks, bands):
    row = lax.broadcasted_iota(jnp.int32, (META, masks.shape[1]), 0)
    return jnp.where(row == 0, masks, jnp.where(row == 1, bands, 0.0)).astype(BF16)


def meta_of(ref, cells):
    tail = ref[pl.ds(cells, META), :].astype(F32)
    return tail[0:1, :cells], tail[1:2, :cells]


def in_turn(count, stages):
    state = [None] * count
    for step in range(count + len(stages) - 1):
        for index, stage in enumerate(stages):
            piece = step - index
            if 0 <= piece < count:
                state[piece] = stage(piece, state[piece])


def project(field, gain, attend_in, at, query, key, value):
    rows = pl.ds(at, field.shape[0])
    normed = normalize(field, gain)
    query[rows, :] = (product(normed, attend_in[:, :D]) * QSCALE).astype(BF16)
    key[rows, :] = product(normed, attend_in[:, D : 2 * D]).astype(BF16)
    value[rows, :] = product(normed, attend_in[:, 2 * D :]).astype(BF16)


def set_bias(bias, bands, masks):
    cells = bands.shape[1]
    classes = lax.broadcasted_iota(jnp.int32, (CLASSES, cells), 0).astype(F32)
    one_hot = (classes == bands).astype(F32).astype(BF16)
    same = lax.dot_general(one_hot, one_hot, TRANSPOSED_LEFT, preferred_element_type=F32)
    asking = lax.broadcasted_iota(jnp.int32, (cells, cells), 0)
    asked = lax.broadcasted_iota(jnp.int32, (cells, cells), 1)
    allowed = (same > 0.5) & ((masks > 0.5) | (asking == asked))
    bias[...] = jnp.where(allowed, 0.0, -1e30)


def attend(query, key, value, bias, context, low, count):
    first = lax.broadcasted_iota(jnp.int32, (1, 2 * HD), 1) < HD
    rows = pl.ds(low, count)
    sums = {}

    def lanes(unit):
        return slice(2 * HD * (unit // 2), 2 * HD * (unit // 2 + 1))

    def own(unit, inside, outside):
        return jnp.where(first, inside, outside) if unit % 2 == 0 else jnp.where(first, outside, inside)

    def score(unit, _):
        queries = query[rows, lanes(unit)]
        queries = own(unit, queries, jnp.zeros_like(queries))
        scores = lax.dot_general(
            queries, key[:, lanes(unit)], TRANSPOSED_RIGHT, preferred_element_type=F32
        )
        return scores + bias[rows, :]

    def weigh(unit, scores):
        return jnp.exp2(scores - jnp.max(scores, -1, keepdims=True)).astype(BF16)

    def gather(unit, weights):
        values = value[:, lanes(unit)]
        sums[unit] = product(weights, own(unit, values, jnp.ones_like(values)))
        if unit % 2 == 1:
            even, odd = sums.pop(unit - 1), sums.pop(unit)
            above = jnp.where(first, even, odd)
            below = pltpu.roll(jnp.where(first, odd, even), HD, 1)
            context[rows, lanes(unit)] = (above / below).astype(BF16)

    in_turn(H, (score, weigh, gather))


def finish(fields, context, lows, attend_out, gain, expand, contract, write):
    def start(index, _):
        rows = pl.ds(lows[index], fields[index].shape[0])
        added = fields[index] + product(context[rows, :], attend_out[...])
        resid = added.astype(BF16).astype(F32)
        return resid, normalize(resid, gain)

    def widen(index, state):
        return state[0], product(state[1], expand[...])

    def bend(index, state):
        return state[0], gelu(state[1]).astype(BF16)

    def end(index, state):
        write(index, state[0] + product(state[1], contract[...]))

    in_turn(len(fields), (start, widen, bend, end))


def pack_main_kernel(block_hbm, valid_hbm, main, token, block, valid, sems):
    height = block_hbm.shape[0]
    rows = height - 2 * SH
    copies = (
        pltpu.make_async_copy(valid_hbm, valid, sems.at[0]),
        pltpu.make_async_copy(block_hbm.at[pl.ds(SH, rows)], block, sems.at[1]),
    )
    for copy in copies:
        copy.start()
    token[...] = jnp.zeros_like(token)
    copies[0].wait()
    masks = mask_lanes(valid, SH, 0, D)
    main[pl.ds(rows * SW, META), :] = meta_rows(masks, jnp.zeros_like(masks))
    copies[1].wait()
    main[pl.ds(0, rows * SW), :] = half_columns(block[...], 0).astype(BF16)


def early_kernel(
    block, bands, valid, token, gains, attend_in,
    side, corner, row_end, cells_here, query, key, value, notes,
):
    height = block.shape[0]
    part = SH * SW
    for out, low, column in ((side, height - SH, 0), (corner, 0, 0), (row_end, 0, SW)):
        out[pl.ds(0, part), :] = half_columns(block[low : low + SH], column).astype(BF16)
        masks = mask_lanes(valid, low, column, D)
        out[pl.ds(part, META), :] = meta_rows(masks, band_lanes(bands, low, SH, D))
    local = half_columns(block[SH:], SW)
    cells_here[...] = local.astype(BF16)
    window_notes = [
        (band_lanes(bands, SH, height - SH, D), mask_lanes(valid, SH, SW, D)),
    ]
    for row in range(0, height, WH):
        row_bands = band_lanes(bands, row, WH, 2 * part)
        window_notes.append((
            jnp.concatenate([row_bands, row_bands], 1),
            jnp.concatenate(
                [mask_lanes(valid, row, SW, 2 * part), mask_lanes(valid, row, 0, 2 * part)], 1
            ),
        ))
    for index, pair in enumerate(window_notes):
        for offset, lanes in enumerate(pair):
            notes[pl.ds(2 * index + offset, 1), :] = lanes
    project(local, gains[0, 0:1], attend_in, 0, query, key, value)


def window_a_kernel(
    cells_here, notes, taken, near_query, near_key, near_value,
    gains, attend_in, attend_out, expand, contract,
    away, home, query, key, value, bias, context,
):
    cells = away.shape[0]
    for near, whole in ((near_query, query), (near_key, key), (near_value, value)):
        whole[pl.ds(0, cells), :] = near[pl.ds(0, cells), :]
    local = cells_here[pl.ds(0, cells), :].astype(F32)
    remote = taken[pl.ds(0, cells), :].astype(F32)
    project(remote, gains[0, 0:1], attend_in, cells, query, key, value)
    row_bands = notes[0:1, :cells]
    masks, _ = meta_of(taken, cells)
    set_bias(
        bias,
        jnp.concatenate([row_bands, row_bands], 1),
        jnp.concatenate([notes[1:2, :cells], masks], 1),
    )
    attend(query, key, value, bias, context, 0, 2 * cells)

    def write(index, out):
        (home, away)[index][...] = out.astype(BF16)

    finish([local, remote], context, (0, cells), attend_out, gains[0, 1:2], expand, contract, write)


def window_b_away_kernel(
    window_a_first, notes, taken_side, taken_corner, taken_end, near_query, near_key, near_value,
    gains, attend_in, attend_out, expand, contract,
    away_side, away_corner, home_end, query, key, value, bias, context,
):
    cells = away_side.shape[0]
    skip = near_query.shape[0] - cells
    for near, whole in ((near_query, query), (near_key, key), (near_value, value)):
        whole[pl.ds(0, cells), :] = near[pl.ds(skip, cells), :]
    fields = []
    bands_here = [notes[0:1, skip : skip + cells]]
    masks_here = [notes[1:2, skip : skip + cells]]
    for taken in (taken_end, taken_side, taken_corner):
        fields.append(taken[pl.ds(0, cells), :].astype(F32))
        masks, row_bands = meta_of(taken, cells)
        masks_here.append(masks)
        bands_here.append(row_bands)
    bands_here[2] = bands_here[0]
    project(jnp.concatenate(fields, 0), gains[0, 0:1], attend_in, cells, query, key, value)
    set_bias(bias, jnp.concatenate(bands_here, 1), jnp.concatenate(masks_here, 1))
    attend(query, key, value, bias, context, cells, 3 * cells)

    def write(index, out):
        out = out.astype(BF16)
        if index == 0:
            away_side[...], away_corner[...] = out[:cells], out[cells:]
        else:
            home_end[...] = out

    fields = [jnp.concatenate(fields[1:], 0), fields[0]]
    finish(fields, context, (2 * cells, cells), attend_out, gains[0, 1:2], expand, contract, write)


def between_kernel(
    cells_here, query, key, value, bias, gains, attend_out, expand, contract,
    home, far, notes, next_gains, attend_in_hbm, attend_out_hbm, expand_hbm, contract_hbm,
    home_side, next_query, next_key, next_value, next_bias,
    next_attend_in, next_attend_out, next_expand, next_contract, context, sems,
):
    loads = (
        (attend_in_hbm, next_attend_in), (attend_out_hbm, next_attend_out),
        (expand_hbm, next_expand), (contract_hbm, next_contract),
    )
    copies = [
        pltpu.make_async_copy(source.at[1], target, sems.at[index])
        for index, (source, target) in enumerate(loads)
    ]
    for copy in copies:
        copy.start()
    part = home_side.shape[0]
    attend(query, key, value, bias, context, 0, part)
    near = cells_here[pl.ds(cells_here.shape[0] - part, part), :]
    kept = []

    def write(index, out):
        home_side[...] = out.astype(BF16)
        kept.append(out.astype(BF16).astype(F32))

    finish([near.astype(F32)], context, (0,), attend_out, gains[0, 1:2], expand, contract, write)
    for index in range(2):
        set_bias(next_bias.at[index], notes[2 * index + 2 : 2 * index + 3],
                 notes[2 * index + 3 : 2 * index + 4])
    pieces = ((0, part, home[:part].astype(F32)),
              (0, 3 * part, far[:part].astype(F32)),
              (1, 0, jnp.concatenate([home[part:].astype(F32), kept[0], far[part:].astype(F32)], 0)))
    copies[0].wait()
    for index, at, field in pieces:
        project(field, next_gains[1, 0:1], next_attend_in, at,
                next_query.at[index], next_key.at[index], next_value.at[index])
    for copy in copies[1:]:
        copy.wait()


def second_kernel(
    home, home_side, far, far_side, far_corner, near_end,
    early_query, early_key, early_value, bias,
    gains, attend_in, attend_out, expand, contract,
    out_hbm, query, key, value, context, out_ref, sems,
):
    part = SH * SW
    copies = []
    low, high = slice(0, part), slice(part, 2 * part)
    windows = (
        (near_end[...], home[low], far_corner[...], far[low]),
        (home[high], home_side[...], far[high], far_side[...]),
    )
    windows = [[piece.astype(F32) for piece in parts] for parts in windows]
    pieces = ((0, 0, windows[0][0]), (0, 2 * part, windows[0][2]), (1, 3 * part, windows[1][3]))
    for index, at, field in pieces:
        project(field, gains[1, 0:1], attend_in, at, query.at[index], key.at[index], value.at[index])
    for index in range(len(windows)):
        attend(
            query.at[index], key.at[index], value.at[index], bias.at[index],
            context.at[pl.ds(4 * part * index, 4 * part)], 0, 4 * part,
        )
    fields = [jnp.concatenate(parts[at : at + 2], 0) for parts in windows for at in (0, 2)]
    near = {}

    def write(index, out):
        window = index // 2
        if index % 2 == 0:
            near[window] = out
            return
        both = [piece.reshape(WH, SW, D) for piece in (out, near.pop(window))]
        rows = pl.ds(window * WH, WH)
        out_ref[rows] = jnp.concatenate(both, 1).astype(BF16)
        copies.append(pltpu.make_async_copy(out_ref.at[rows], out_hbm.at[rows], sems.at[window]))
        copies[-1].start()

    lows = [2 * part * at for at in range(len(fields))]
    finish(fields, context, lows, attend_out, gains[1, 1:2], expand, contract, write)
    for copy in copies:
        copy.wait()


def call(kernel, name, shapes, specs, scratch, flops, *operands, limit=32, aliases=(), outs=VMEM):
    size = sum(operand.size * operand.dtype.itemsize for operand in operands)
    shapes = [shape if isinstance(shape, jax.ShapeDtypeStruct) else jax.ShapeDtypeStruct(shape, BF16)
              for shape in shapes]
    return pl.pallas_call(
        kernel,
        out_shape=shapes,
        in_specs=specs,
        out_specs=[outs] + [VMEM] * (len(shapes) - 1),
        scratch_shapes=scratch,
        compiler_params=pltpu.CompilerParams(vmem_limit_bytes=limit * 2**20),
        cost_estimate=pl.CostEstimate(flops=flops, bytes_accessed=size, transcendentals=0),
        input_output_aliases=dict(aliases),
        name=name,
    )(*operands)


def on_device(
    atmosphere, pole_band, key_valid, norm_gains, attend_in, attend_out, expand, contract
):
    height, breadth = atmosphere.shape[0], atmosphere.shape[1]
    assert height == 2 * WH and breadth == WW
    lons, lats = lax.axis_size("lon"), lax.axis_size("lat")

    def moved(value, lon_step, lat_step):
        pairs = [
            (lon * lats + lat, (lon + lon_step) % lons * lats + (lat + lat_step) % lats)
            for lon in range(lons)
            for lat in range(lats)
        ]
        return lax.ppermute(value, ("lon", "lat"), pairs)

    cells = WH * WW
    half, quarter = cells // 2, cells // 4
    wide = pltpu.VMEM((cells, D), BF16)
    bias_shape = jax.ShapeDtypeStruct((cells, cells), F32)
    bias_scratch = pltpu.VMEM((cells, cells), F32)
    hidden = expand.shape[-1]
    each = 2 * D * 3 * D
    flops = cells * 2 * D * (D + 2 * hidden) + 4 * cells * cells * D

    valid = key_valid.T
    valid_scratch = pltpu.VMEM(valid.shape, valid.dtype)
    main, token = call(
        pack_main_kernel, "pack_main", [(half + META, D), (META, 2 * HD)], [HBM] * 2,
        [pltpu.VMEM((WH, breadth, D), BF16), valid_scratch, pltpu.SemaphoreType.DMA((2,))],
        10**6, atmosphere, valid, limit=62,
    )
    far_main = moved(main, -1, 0)

    weights = [
        (norm_gains, attend_in[0], attend_out[0], expand[0], contract[0]),
        (norm_gains, attend_in, attend_out, expand, contract),
    ]
    side, corner, row_end, here, *near, notes = call(
        early_kernel, "early",
        [(quarter + META, D)] * 3 + [(half + quarter, D)] * 4
        + [jax.ShapeDtypeStruct((META, D), F32)],
        [VMEM, SMEM] + [VMEM] * 4, [], each * (half + quarter),
        atmosphere, pole_band, valid, token, *weights[0][:2],
    )
    far_side = moved(side, -1, 0)
    far_corner = moved(corner, -1, -1)
    near_end = moved(row_end, 0, -1)

    away, home = call(
        window_a_kernel, "window_a", [(half, D)] * 2, [VMEM] * 11,
        [wide] * 3 + [bias_scratch, wide], flops + each * half,
        here, notes, far_main, *near, *weights[0],
    )
    back_main = moved(away, 1, 0)
    away_side, away_corner, home_end, *inside = call(
        window_b_away_kernel, "window_b_away",
        [(quarter, D)] * 3 + [(cells, D)] * 3 + [bias_shape], [VMEM] * 13,
        [wide], 3 * flops // 4 + each * 3 * quarter,
        home, notes, far_side, far_corner, near_end, *near, *weights[0],
    )
    pair = (2, cells, D)
    home_side, *inside = call(
        between_kernel, "between",
        [(quarter, D)] + [pair] * 3 + [jax.ShapeDtypeStruct((2, cells, cells), F32)]
        + [array.shape[1:] for array in weights[1][1:]],
        [VMEM] * 13 + [HBM] * 4, [wide, pltpu.SemaphoreType.DMA((4,))], flops // 4 + each * 5 * quarter,
        here, *inside, weights[0][0], *weights[0][2:],
        home, back_main, notes, *weights[1],
    )
    back_side = moved(away_side, 1, 0)
    back_corner = moved(away_corner, 1, 1)
    back_end = moved(home_end, 0, 1)
    return call(
        second_kernel, "second", [(height, breadth, D)] + [pair] * 3, [VMEM] * 15,
        [pltpu.VMEM((2 * cells, D), BF16), pltpu.VMEM(atmosphere.shape, BF16),
         pltpu.SemaphoreType.DMA((2,))],
        2 * flops + each * 5 * quarter,
        home, home_side, back_main, back_side, back_corner, back_end, *inside[:4], norm_gains, *inside[4:],
        aliases=((6, 1), (7, 2), (8, 3)), outs=HBM,
    )[0]


def solution(mesh):
    in_specs = (
        P(("groups", "lat"), "lon", None),
        P(("groups", "lat")),
        P(("groups", "lat"), "lon"),
        P(),
        P(),
        P(),
        P(),
        P(),
    )
    out_specs = P(("groups", "lat"), "lon", None)
    return jax.shard_map(
        on_device, mesh=mesh, in_specs=in_specs, out_specs=out_specs, check_vma=False
    )
```

```python
import functools
import math

import jax
import jax.numpy as jnp
from jax import lax
from jax.experimental import pallas as pl
from jax.experimental.pallas import tpu as pltpu
from jax.sharding import PartitionSpec as P

D = 512
H = 8
WH = 32
WW = 16
HD = 64
SH = 16
SW = 8

norm_eps = 1e-05

F32 = jnp.float32
BF16 = jnp.bfloat16
CLASSES = 128
META = 16
CHUNKS = 4
QSCALE = math.log2(math.e) / math.sqrt(HD)
TRANSPOSED_RIGHT = (((1,), (1,)), ((), ()))
TRANSPOSED_LEFT = (((0,), (0,)), ((), ()))
VMEM = pl.BlockSpec(memory_space=pltpu.VMEM)
SMEM = pl.BlockSpec(memory_space=pltpu.SMEM)
HBM = pl.BlockSpec(memory_space=pltpu.HBM)


def product(left, right):
    return jnp.dot(left, right, preferred_element_type=F32)


def normalize(field, gains):
    average = jnp.mean(field, -1, keepdims=True)
    centred = field - average
    spread = jnp.mean(centred * centred, -1, keepdims=True)
    return (centred * lax.rsqrt(spread + norm_eps) * gains).astype(BF16)


def gelu(value):
    scale = math.sqrt(2.0 / math.pi)
    bent = jnp.tanh(value * (scale + (scale * 0.044715) * (value * value)))
    half = 0.5 * value
    return half + half * bent


def half_columns(block, start):
    part = block.astype(F32)[:, start : start + SW]
    return part.reshape(block.shape[0] * SW, D)


def mask_lanes(valid, low, start, lanes):
    columns, height = valid.shape
    row = lax.broadcasted_iota(jnp.int32, (height, lanes), 0)
    cell = lax.broadcasted_iota(jnp.int32, (height, lanes), 1)
    pick = (row == low + lax.div(cell, SW)).astype(F32).astype(BF16)
    spread = product(valid[...].astype(F32).astype(BF16), pick)
    column = lax.broadcasted_iota(jnp.int32, (columns, lanes), 0)
    own = start + lax.rem(lax.broadcasted_iota(jnp.int32, (columns, lanes), 1), SW)
    return jnp.sum(jnp.where(column == own, spread, 0.0), 0, keepdims=True)


def band_lanes(bands, start, rows, lanes):
    own = lax.div(lax.broadcasted_iota(jnp.int32, (1, lanes), 1), SW)
    found = jnp.zeros((1, lanes), jnp.int32)
    for row in range(rows):
        found = jnp.where(own == row, bands[start + row], found)
    return found.astype(F32)


def meta_rows(masks, bands):
    row = lax.broadcasted_iota(jnp.int32, (META, masks.shape[1]), 0)
    return jnp.where(row == 0, masks, jnp.where(row == 1, bands, 0.0)).astype(BF16)


def meta_of(ref, cells):
    tail = ref[pl.ds(cells, META), :].astype(F32)
    return tail[0:1, :cells], tail[1:2, :cells]


def in_turn(count, stages):
    state = [None] * count
    for step in range(count + len(stages) - 1):
        for index, stage in enumerate(stages):
            piece = step - index
            if 0 <= piece < count:
                state[piece] = stage(piece, state[piece])


def project(field, gain, attend_in, *places):
    normed = normalize(field, gain)
    for kind in range(3):
        result = product(normed, attend_in[:, kind * D : (kind + 1) * D])
        result = (result * QSCALE if kind == 0 else result).astype(BF16)
        done = 0
        for refs, at, count in places:
            refs[kind][pl.ds(at, count), :] = result[done : done + count]
            done += count


def set_bias(bias, bands, masks):
    cells = bands.shape[1]
    classes = lax.broadcasted_iota(jnp.int32, (CLASSES, cells), 0).astype(F32)
    one_hot = (classes == bands).astype(F32).astype(BF16)
    same = lax.dot_general(one_hot, one_hot, TRANSPOSED_LEFT, preferred_element_type=F32)
    asking = lax.broadcasted_iota(jnp.int32, (cells, cells), 0)
    asked = lax.broadcasted_iota(jnp.int32, (cells, cells), 1)
    allowed = (same > 0.5) & ((masks > 0.5) | (asking == asked))
    bias[...] = jnp.where(allowed, 0.0, -1e30)


def attend(query, key, value, bias, context, low, count):
    first = lax.broadcasted_iota(jnp.int32, (1, 2 * HD), 1) < HD
    rows = pl.ds(low, count)
    sums = {}

    def lanes(unit):
        return slice(2 * HD * (unit // 2), 2 * HD * (unit // 2 + 1))

    def own(unit, inside, outside):
        return jnp.where(first, inside, outside) if unit % 2 == 0 else jnp.where(first, outside, inside)

    def score(unit, _):
        queries = query[rows, lanes(unit)]
        queries = own(unit, queries, jnp.zeros_like(queries))
        scores = lax.dot_general(
            queries, key[:, lanes(unit)], TRANSPOSED_RIGHT, preferred_element_type=F32
        )
        return scores + bias[rows, :]

    def weigh(unit, scores):
        return jnp.exp2(scores - jnp.max(scores, -1, keepdims=True)).astype(BF16)

    def gather(unit, weights):
        values = value[:, lanes(unit)]
        sums[unit] = product(weights, own(unit, values, jnp.ones_like(values)))
        if unit % 2 == 1:
            even, odd = sums.pop(unit - 1), sums.pop(unit)
            above = jnp.where(first, even, odd)
            below = pltpu.roll(jnp.where(first, odd, even), HD, 1)
            context[rows, lanes(unit)] = (above / below).astype(BF16)

    in_turn(H, (score, weigh, gather))


def finish(fields, context, lows, attend_out, gain, expand, contract, write):
    def start(index, _):
        rows = pl.ds(lows[index], fields[index].shape[0])
        added = fields[index] + product(context[rows, :], attend_out[...])
        resid = added.astype(BF16).astype(F32)
        return resid, normalize(resid, gain)

    def widen(index, state):
        return state[0], product(state[1], expand[...])

    def bend(index, state):
        return state[0], gelu(state[1]).astype(BF16)

    def end(index, state):
        write(index, state[0] + product(state[1], contract[...]))

    in_turn(len(fields), (start, widen, bend, end))


def pack_main_kernel(block_hbm, valid_hbm, main_hbm, token, block, valid, main, in_sems, out_sems):
    rows = block.shape[0]
    cells = rows * SW
    chunk = rows // CHUNKS
    loads = [
        pltpu.make_async_copy(
            block_hbm.at[pl.ds(SH + at * chunk, chunk)], block.at[pl.ds(at * chunk, chunk)],
            in_sems.at[at],
        )
        for at in range(CHUNKS)
    ]
    stores = [
        pltpu.make_async_copy(main.at[part], main_hbm.at[part], out_sems.at[at])
        for at, part in enumerate(
            [pl.ds(at * chunk * SW, chunk * SW) for at in range(CHUNKS)] + [pl.ds(cells, META)]
        )
    ]
    load_valid = pltpu.make_async_copy(valid_hbm, valid, in_sems.at[CHUNKS])
    load_valid.start()
    for load in loads:
        load.start()
    token[...] = jnp.zeros_like(token)
    load_valid.wait()
    masks = mask_lanes(valid, SH, 0, D)
    main[pl.ds(cells, META), :] = meta_rows(masks, jnp.zeros_like(masks))
    stores[CHUNKS].start()
    for at in range(CHUNKS):
        loads[at].wait()
        part = half_columns(block[pl.ds(at * chunk, chunk)], 0)
        main[pl.ds(at * chunk * SW, chunk * SW), :] = part.astype(BF16)
        stores[at].start()
    for store in stores:
        store.wait()


def pack_rest_kernel(
    block_hbm, bands_hbm, valid_hbm, token_hbm, side, corner, row_end,
    block, bands, valid, sems,
):
    height = block_hbm.shape[0]
    part = SH * SW
    copies = [
        pltpu.make_async_copy(source, target, sems.at[index])
        for index, (source, target) in enumerate((
            (bands_hbm, bands), (valid_hbm, valid),
            (block_hbm.at[pl.ds(0, SH)], block.at[0]),
            (block_hbm.at[pl.ds(height - SH, SH)], block.at[1]),
        ))
    ]
    for copy in copies:
        copy.start()
    places = ((side, height - SH, 1, 0), (corner, 0, 0, 0), (row_end, 0, 0, SW))
    for copy in copies[:2]:
        copy.wait()
    for out, low, _, column in places:
        masks = mask_lanes(valid, low, column, D)
        out[pl.ds(part, META), :] = meta_rows(masks, band_lanes(bands, low, SH, D))
    for copy in copies[2:]:
        copy.wait()
    for out, _, which, column in places:
        out[pl.ds(0, part), :] = half_columns(block[which], column).astype(BF16)


def near_kernel(
    block, bands, valid, gains, attend_in, cells_here, query, key, value, notes,
):
    height = block.shape[0]
    part = SH * SW
    local = half_columns(block[SH:], SW)
    cells_here[...] = local.astype(BF16)
    window_notes = [
        (band_lanes(bands, SH, height - SH, D), mask_lanes(valid, SH, SW, D)),
    ]
    for row in range(0, height, WH):
        row_bands = band_lanes(bands, row, WH, 2 * part)
        window_notes.append((
            jnp.concatenate([row_bands, row_bands], 1),
            jnp.concatenate(
                [mask_lanes(valid, row, SW, 2 * part), mask_lanes(valid, row, 0, 2 * part)], 1
            ),
        ))
    for index, pair in enumerate(window_notes):
        for offset, lanes in enumerate(pair):
            notes[pl.ds(2 * index + offset, 1), :] = lanes
    project(local, gains[0, 0:1], attend_in, ((query, key, value), 0, local.shape[0]))


def window_a_kernel(
    cells_here, notes, taken, near_query, near_key, near_value,
    gains, attend_in, attend_out, expand, contract,
    away, home, query, key, value, bias, context,
):
    cells = away.shape[0]
    for near, whole in ((near_query, query), (near_key, key), (near_value, value)):
        whole[pl.ds(0, cells), :] = near[pl.ds(0, cells), :]
    local = cells_here[pl.ds(0, cells), :].astype(F32)
    remote = taken[pl.ds(0, cells), :].astype(F32)
    project(remote, gains[0, 0:1], attend_in, ((query, key, value), cells, cells))
    row_bands = notes[0:1, :cells]
    masks, _ = meta_of(taken, cells)
    set_bias(
        bias,
        jnp.concatenate([row_bands, row_bands], 1),
        jnp.concatenate([notes[1:2, :cells], masks], 1),
    )
    attend(query, key, value, bias, context, 0, 2 * cells)

    def write(index, out):
        (home, away)[index][...] = out.astype(BF16)

    finish([local, remote], context, (0, cells), attend_out, gains[0, 1:2], expand, contract, write)


def window_b_away_kernel(
    window_a_first, notes, taken_side, taken_corner, taken_end, near_query, near_key, near_value,
    gains, attend_in, attend_out, expand, contract,
    away_side, away_corner, home_end, query, key, value, bias, context,
):
    cells = away_side.shape[0]
    skip = near_query.shape[0] - cells
    for near, whole in ((near_query, query), (near_key, key), (near_value, value)):
        whole[pl.ds(0, cells), :] = near[pl.ds(skip, cells), :]
    fields = []
    bands_here = [notes[0:1, skip : skip + cells]]
    masks_here = [notes[1:2, skip : skip + cells]]
    for taken in (taken_end, taken_side, taken_corner):
        fields.append(taken[pl.ds(0, cells), :].astype(F32))
        masks, row_bands = meta_of(taken, cells)
        masks_here.append(masks)
        bands_here.append(row_bands)
    bands_here[2] = bands_here[0]
    project(
        jnp.concatenate(fields, 0), gains[0, 0:1], attend_in,
        ((query, key, value), cells, 3 * cells),
    )
    set_bias(bias, jnp.concatenate(bands_here, 1), jnp.concatenate(masks_here, 1))
    attend(query, key, value, bias, context, cells, 3 * cells)

    def write(index, out):
        out = out.astype(BF16)
        if index == 0:
            away_side[...], away_corner[...] = out[:cells], out[cells:]
        else:
            home_end[...] = out

    fields = [jnp.concatenate(fields[1:], 0), fields[0]]
    finish(fields, context, (2 * cells, cells), attend_out, gains[0, 1:2], expand, contract, write)


def between_kernel(
    cells_here, query, key, value, bias, gains, attend_out, expand, contract,
    home, far, notes, next_gains, attend_in_hbm, attend_out_hbm, expand_hbm, contract_hbm,
    home_side, next_query, next_key, next_value, next_bias,
    next_attend_in, next_attend_out, next_expand, next_contract, context, sems,
):
    loads = (
        (attend_in_hbm, next_attend_in), (attend_out_hbm, next_attend_out),
        (expand_hbm, next_expand), (contract_hbm, next_contract),
    )
    copies = [
        pltpu.make_async_copy(source.at[1], target, sems.at[index])
        for index, (source, target) in enumerate(loads)
    ]
    for copy in copies:
        copy.start()
    part = home_side.shape[0]
    attend(query, key, value, bias, context, 0, part)
    near = cells_here[pl.ds(cells_here.shape[0] - part, part), :]
    kept = []

    def write(index, out):
        home_side[...] = out.astype(BF16)
        kept.append(out.astype(BF16).astype(F32))

    finish([near.astype(F32)], context, (0,), attend_out, gains[0, 1:2], expand, contract, write)
    for index in range(2):
        set_bias(next_bias.at[index], notes[2 * index + 2 : 2 * index + 3],
                 notes[2 * index + 3 : 2 * index + 4])
    copies[0].wait()
    windows = [(next_query.at[at], next_key.at[at], next_value.at[at]) for at in range(2)]
    field = [home[:part], far[:part], home[part:]]
    field = [piece.astype(F32) for piece in field] + [kept[0], far[part:].astype(F32)]
    project(
        jnp.concatenate(field, 0), next_gains[1, 0:1], next_attend_in,
        (windows[0], part, part), (windows[0], 3 * part, part), (windows[1], 0, 3 * part),
    )
    for copy in copies[1:]:
        copy.wait()


def second_kernel(
    home, home_side, far, far_side, far_corner, near_end,
    early_query, early_key, early_value, bias,
    gains, attend_in, attend_out, expand, contract,
    out_hbm, query, key, value, context, out_ref, sems,
):
    part = SH * SW
    copies = []
    low, high = slice(0, part), slice(part, 2 * part)
    windows = (
        (near_end[...], home[low], far_corner[...], far[low]),
        (home[high], home_side[...], far[high], far_side[...]),
    )
    windows = [[piece.astype(F32) for piece in parts] for parts in windows]
    refs = [(query.at[at], key.at[at], value.at[at]) for at in range(2)]
    project(
        jnp.concatenate([windows[0][0], windows[0][2], windows[1][3]], 0),
        gains[1, 0:1], attend_in,
        (refs[0], 0, part), (refs[0], 2 * part, part), (refs[1], 3 * part, part),
    )
    for index in range(len(windows)):
        attend(
            query.at[index], key.at[index], value.at[index], bias.at[index],
            context.at[pl.ds(4 * part * index, 4 * part)], 0, 4 * part,
        )
    fields = [jnp.concatenate(parts[at : at + 2], 0) for parts in windows for at in (0, 2)]
    near = {}

    def write(index, out):
        window = index // 2
        if index % 2 == 0:
            near[window] = out
            return
        both = [piece.reshape(WH, SW, D) for piece in (out, near.pop(window))]
        rows = pl.ds(window * WH, WH)
        out_ref[rows] = jnp.concatenate(both, 1).astype(BF16)
        copies.append(pltpu.make_async_copy(out_ref.at[rows], out_hbm.at[rows], sems.at[window]))
        copies[-1].start()

    lows = [2 * part * at for at in range(len(fields))]
    finish(fields, context, lows, attend_out, gains[1, 1:2], expand, contract, write)
    for copy in copies:
        copy.wait()


def call(kernel, name, shapes, specs, scratch, flops, *operands, limit=32, aliases=(), outs=VMEM):
    size = sum(operand.size * operand.dtype.itemsize for operand in operands)
    shapes = [shape if isinstance(shape, jax.ShapeDtypeStruct) else jax.ShapeDtypeStruct(shape, BF16)
              for shape in shapes]
    return pl.pallas_call(
        kernel,
        out_shape=shapes,
        in_specs=specs,
        out_specs=[outs] + [VMEM] * (len(shapes) - 1),
        scratch_shapes=scratch,
        compiler_params=pltpu.CompilerParams(vmem_limit_bytes=limit * 2**20),
        cost_estimate=pl.CostEstimate(flops=flops, bytes_accessed=size, transcendentals=0),
        input_output_aliases=dict(aliases),
        name=name,
    )(*operands)


def on_device(
    atmosphere, pole_band, key_valid, norm_gains, attend_in, attend_out, expand, contract
):
    height, breadth = atmosphere.shape[0], atmosphere.shape[1]
    assert height == 2 * WH and breadth == WW
    lons, lats = lax.axis_size("lon"), lax.axis_size("lat")

    def moved(value, lon_step, lat_step):
        pairs = [
            (lon * lats + lat, (lon + lon_step) % lons * lats + (lat + lat_step) % lats)
            for lon in range(lons)
            for lat in range(lats)
        ]
        return lax.ppermute(value, ("lon", "lat"), pairs)

    cells = WH * WW
    half, quarter = cells // 2, cells // 4
    wide = pltpu.VMEM((cells, D), BF16)
    bias_shape = jax.ShapeDtypeStruct((cells, cells), F32)
    bias_scratch = pltpu.VMEM((cells, cells), F32)
    hidden = expand.shape[-1]
    each = 2 * D * 3 * D
    flops = cells * 2 * D * (D + 2 * hidden) + 4 * cells * cells * D

    valid = key_valid.T
    valid_scratch = pltpu.VMEM(valid.shape, valid.dtype)
    main, token = call(
        pack_main_kernel, "pack_main", [(half + META, D), (META, 2 * HD)], [HBM] * 2,
        [pltpu.VMEM((WH, breadth, D), BF16), valid_scratch, pltpu.VMEM((half + META, D), BF16),
         pltpu.SemaphoreType.DMA((CHUNKS + 1,)), pltpu.SemaphoreType.DMA((CHUNKS + 1,))],
        10**6, atmosphere, valid, limit=62, outs=HBM,
    )
    far_main = moved(main, -1, 0)

    weights = [
        (norm_gains, attend_in[0], attend_out[0], expand[0], contract[0]),
        (norm_gains, attend_in, attend_out, expand, contract),
    ]
    place = (atmosphere, pole_band, valid)
    side, corner, row_end = call(
        pack_rest_kernel, "pack_rest", [(quarter + META, D)] * 3,
        [HBM] * 4,
        [pltpu.VMEM((2, SH, breadth, D), BF16), pltpu.SMEM(pole_band.shape, pole_band.dtype),
         valid_scratch, pltpu.SemaphoreType.DMA((4,))],
        10**6, *place, token, limit=62,
    )
    far_side = moved(side, -1, 0)
    far_corner = moved(corner, -1, -1)
    near_end = moved(row_end, 0, -1)

    here, *near, notes = call(
        near_kernel, "near",
        [(half + quarter, D)] * 4 + [jax.ShapeDtypeStruct((META, D), F32)],
        [VMEM, SMEM] + [VMEM] * 3, [], each * (half + quarter),
        *place, *weights[0][:2],
    )
    away, home = call(
        window_a_kernel, "window_a", [(half, D)] * 2, [VMEM] * 11,
        [wide] * 3 + [bias_scratch, wide], flops + each * half,
        here, notes, far_main, *near, *weights[0],
    )
    back_main = moved(away, 1, 0)
    away_side, away_corner, home_end, *inside = call(
        window_b_away_kernel, "window_b_away",
        [(quarter, D)] * 3 + [(cells, D)] * 3 + [bias_shape], [VMEM] * 13,
        [wide], 3 * flops // 4 + each * 3 * quarter,
        home, notes, far_side, far_corner, near_end, *near, *weights[0],
    )
    pair = (2, cells, D)
    home_side, *inside = call(
        between_kernel, "between",
        [(quarter, D)] + [pair] * 3 + [jax.ShapeDtypeStruct((2, cells, cells), F32)]
        + [array.shape[1:] for array in weights[1][1:]],
        [VMEM] * 13 + [HBM] * 4, [wide, pltpu.SemaphoreType.DMA((4,))], flops // 4 + each * 5 * quarter,
        here, *inside, weights[0][0], *weights[0][2:],
        home, back_main, notes, *weights[1],
    )
    back_side = moved(away_side, 1, 0)
    back_corner = moved(away_corner, 1, 1)
    back_end = moved(home_end, 0, 1)
    return call(
        second_kernel, "second", [(height, breadth, D)] + [pair] * 3, [VMEM] * 15,
        [pltpu.VMEM((2 * cells, D), BF16), pltpu.VMEM(atmosphere.shape, BF16),
         pltpu.SemaphoreType.DMA((2,))],
        2 * flops + each * 5 * quarter,
        home, home_side, back_main, back_side, back_corner, back_end, *inside[:4], norm_gains, *inside[4:],
        aliases=((6, 1), (7, 2), (8, 3)), outs=HBM,
    )[0]


def solution(mesh):
    in_specs = (
        P(("groups", "lat"), "lon", None),
        P(("groups", "lat")),
        P(("groups", "lat"), "lon"),
        P(),
        P(),
        P(),
        P(),
        P(),
    )
    out_specs = P(("groups", "lat"), "lon", None)
    return jax.shard_map(
        on_device, mesh=mesh, in_specs=in_specs, out_specs=out_specs, check_vma=False
    )
```

```python
import functools
import math

import jax
import jax.numpy as jnp
from jax import lax
from jax.experimental import pallas as pl
from jax.experimental.pallas import tpu as pltpu
from jax.sharding import PartitionSpec as P

D = 512
H = 8
WH = 32
WW = 16
HD = 64
SH = 16
SW = 8

norm_eps = 1e-05

F32 = jnp.float32
BF16 = jnp.bfloat16
CLASSES = 128
META = 16
QSCALE = math.log2(math.e) / math.sqrt(HD)
TRANSPOSED_RIGHT = (((1,), (1,)), ((), ()))
TRANSPOSED_LEFT = (((0,), (0,)), ((), ()))
VMEM = pl.BlockSpec(memory_space=pltpu.VMEM)
SMEM = pl.BlockSpec(memory_space=pltpu.SMEM)
HBM = pl.BlockSpec(memory_space=pltpu.HBM)


def product(left, right):
    return jnp.dot(left, right, preferred_element_type=F32)


def normalize(field, gains):
    average = jnp.mean(field, -1, keepdims=True)
    centred = field - average
    spread = jnp.mean(centred * centred, -1, keepdims=True)
    return (centred * lax.rsqrt(spread + norm_eps) * gains).astype(BF16)


def gelu(value):
    scale = math.sqrt(2.0 / math.pi)
    bent = jnp.tanh(value * (scale + (scale * 0.044715) * (value * value)))
    half = 0.5 * value
    return half + half * bent


def half_columns(block, start):
    part = block.astype(F32)[:, start : start + SW]
    return part.reshape(block.shape[0] * SW, D)


def mask_lanes(valid, low, start, lanes):
    columns, height = valid.shape
    row = lax.broadcasted_iota(jnp.int32, (height, lanes), 0)
    cell = lax.broadcasted_iota(jnp.int32, (height, lanes), 1)
    pick = (row == low + lax.div(cell, SW)).astype(F32).astype(BF16)
    spread = product(valid[...].astype(F32).astype(BF16), pick)
    column = lax.broadcasted_iota(jnp.int32, (columns, lanes), 0)
    own = start + lax.rem(lax.broadcasted_iota(jnp.int32, (columns, lanes), 1), SW)
    return jnp.sum(jnp.where(column == own, spread, 0.0), 0, keepdims=True)


def band_lanes(bands, start, rows, lanes):
    own = lax.div(lax.broadcasted_iota(jnp.int32, (1, lanes), 1), SW)
    found = jnp.zeros((1, lanes), jnp.int32)
    for row in range(rows):
        found = jnp.where(own == row, bands[start + row], found)
    return found.astype(F32)


def meta_rows(masks, bands):
    row = lax.broadcasted_iota(jnp.int32, (META, masks.shape[1]), 0)
    return jnp.where(row == 0, masks, jnp.where(row == 1, bands, 0.0)).astype(BF16)


def meta_of(ref, cells):
    tail = ref[pl.ds(cells, META), :].astype(F32)
    return tail[0:1, :cells], tail[1:2, :cells]


def in_turn(count, stages, between=()):
    state = [None] * count
    steps = count + len(stages) - 1
    between = list(between)
    for step in range(steps):
        for _ in range(-(-len(between) // (steps - step))):
            between.pop(0)()
        for index, stage in enumerate(stages):
            piece = step - index
            if 0 <= piece < count:
                state[piece] = stage(piece, state[piece])


def project(field, gain, attend_in, *places):
    normed = normalize(field, gain)
    for kind in range(3):
        result = product(normed, attend_in[:, kind * D : (kind + 1) * D])
        result = (result * QSCALE if kind == 0 else result).astype(BF16)
        done = 0
        for refs, at, count in places:
            refs[kind][pl.ds(at, count), :] = result[done : done + count]
            done += count


def allowed_pairs(bands, masks):
    cells = bands.shape[1]
    classes = lax.broadcasted_iota(jnp.int32, (CLASSES, cells), 0).astype(F32)
    one_hot = (classes == bands).astype(F32).astype(BF16)
    same = lax.dot_general(one_hot, one_hot, TRANSPOSED_LEFT, preferred_element_type=F32)
    asking = lax.broadcasted_iota(jnp.int32, (cells, cells), 0)
    asked = lax.broadcasted_iota(jnp.int32, (cells, cells), 1)
    allowed = (same > 0.5) & ((masks > 0.5) | (asking == asked))
    return jnp.where(allowed, 0.0, -1e30)


def set_bias(bias, bands, masks):
    bias[...] = allowed_pairs(bands, masks)


def attend(query, key, value, bias, context, low, count, between=()):
    first = lax.broadcasted_iota(jnp.int32, (1, 2 * HD), 1) < HD
    rows = pl.ds(low, count)
    sums = {}

    def lanes(unit):
        return slice(2 * HD * (unit // 2), 2 * HD * (unit // 2 + 1))

    def own(unit, inside, outside):
        return jnp.where(first, inside, outside) if unit % 2 == 0 else jnp.where(first, outside, inside)

    def score(unit, _):
        queries = query[rows, lanes(unit)]
        queries = own(unit, queries, jnp.zeros_like(queries))
        scores = lax.dot_general(
            queries, key[:, lanes(unit)], TRANSPOSED_RIGHT, preferred_element_type=F32
        )
        return scores + bias[rows, :]

    def weigh(unit, scores):
        return jnp.exp2(scores - jnp.max(scores, -1, keepdims=True)).astype(BF16)

    def gather(unit, weights):
        values = value[:, lanes(unit)]
        sums[unit] = product(weights, own(unit, values, jnp.ones_like(values)))
        if unit % 2 == 1:
            even, odd = sums.pop(unit - 1), sums.pop(unit)
            above = jnp.where(first, even, odd)
            below = pltpu.roll(jnp.where(first, odd, even), HD, 1)
            context[rows, lanes(unit)] = (above / below).astype(BF16)

    in_turn(H, (score, weigh, gather), between)


def finish(fields, context, lows, attend_out, gain, expand, contract, write):
    def start(index, _):
        rows = pl.ds(lows[index], fields[index].shape[0])
        added = fields[index] + product(context[rows, :], attend_out[...])
        resid = added.astype(BF16).astype(F32)
        return resid, normalize(resid, gain)

    def widen(index, state):
        return state[0], product(state[1], expand[...])

    def bend(index, state):
        return state[0], gelu(state[1]).astype(BF16)

    def end(index, state):
        write(index, state[0] + product(state[1], contract[...]))

    in_turn(len(fields), (start, widen, bend, end))


def finish_steps(fields, context, lows, attend_out, gain, expand, contract, write):
    state = {}

    def start(index):
        rows = pl.ds(lows[index], fields[index].shape[0])
        added = fields[index] + product(context[rows, :], attend_out[...])
        resid = added.astype(BF16).astype(F32)
        state[index] = resid, normalize(resid, gain)

    def widen(index):
        resid, normed = state[index]
        state[index] = resid, product(normed, expand[...])

    def bend(index):
        resid, wide = state[index]
        state[index] = resid, gelu(wide).astype(BF16)

    def end(index):
        resid, hidden = state.pop(index)
        write(index, resid + product(hidden, contract[...]))

    return [
        functools.partial(stage, index)
        for step in range(len(fields) + 3)
        for at, stage in enumerate((start, widen, bend, end))
        for index in [step - at]
        if 0 <= index < len(fields)
    ]


def pack_main_kernel(block_hbm, valid_hbm, main, token, block, valid, sems):
    height = block_hbm.shape[0]
    rows = height - 2 * SH
    copies = (
        pltpu.make_async_copy(valid_hbm, valid, sems.at[0]),
        pltpu.make_async_copy(block_hbm.at[pl.ds(SH, rows)], block, sems.at[1]),
    )
    for copy in copies:
        copy.start()
    token[...] = jnp.zeros_like(token)
    copies[0].wait()
    masks = mask_lanes(valid, SH, 0, D)
    main[pl.ds(rows * SW, META), :] = meta_rows(masks, jnp.zeros_like(masks))
    copies[1].wait()
    main[pl.ds(0, rows * SW), :] = half_columns(block[...], 0).astype(BF16)


def early_kernel(
    block, bands, valid, token, gains, attend_in,
    side, corner, row_end, cells_here, query, key, value, notes,
    first_query, first_key, first_value, first_bias,
):
    height = block.shape[0]
    part = SH * SW
    for out, low, column in ((side, height - SH, 0), (corner, 0, 0), (row_end, 0, SW)):
        out[pl.ds(0, part), :] = half_columns(block[low : low + SH], column).astype(BF16)
        masks = mask_lanes(valid, low, column, D)
        out[pl.ds(part, META), :] = meta_rows(masks, band_lanes(bands, low, SH, D))
    local = half_columns(block[SH:], SW)
    cells_here[...] = local.astype(BF16)
    window_notes = [
        (band_lanes(bands, SH, height - SH, D), mask_lanes(valid, SH, SW, D)),
    ]
    for row in range(0, height, WH):
        row_bands = band_lanes(bands, row, WH, 2 * part)
        window_notes.append((
            jnp.concatenate([row_bands, row_bands], 1),
            jnp.concatenate(
                [mask_lanes(valid, row, SW, 2 * part), mask_lanes(valid, row, 0, 2 * part)], 1
            ),
        ))
    for index, pair in enumerate(window_notes):
        for offset, lanes in enumerate(pair):
            notes[pl.ds(2 * index + offset, 1), :] = lanes
    near = local.shape[0] - part
    project(
        local, gains[0, 0:1], attend_in,
        ((first_query, first_key, first_value), 0, near), ((query, key, value), 0, part),
    )
    row_bands, masks = notes[0:1, :near], notes[1:2, :near]
    set_bias(
        first_bias,
        jnp.concatenate([row_bands, row_bands], 1),
        jnp.concatenate([masks, jnp.ones_like(masks)], 1),
    )


def window_a_kernel(
    cells_here, taken, early_query, early_key, early_value, early_bias,
    gains, attend_in, attend_out, expand, contract,
    away, home, query, key, value, bias, context,
):
    cells = away.shape[0]
    local = cells_here[pl.ds(0, cells), :].astype(F32)
    remote = taken[pl.ds(0, cells), :].astype(F32)
    project(remote, gains[0, 0:1], attend_in, ((query, key, value), cells, cells))
    masks, _ = meta_of(taken, cells)
    columns = bias[:, cells:]
    asking = lax.broadcasted_iota(jnp.int32, columns.shape, 0)
    asked = lax.broadcasted_iota(jnp.int32, columns.shape, 1) + cells
    bias[:, cells:] = jnp.where((masks > 0.5) | (asking == asked), columns, -1e30)
    attend(query, key, value, bias, context, 0, 2 * cells)

    def write(index, out):
        (home, away)[index][...] = out.astype(BF16)

    finish([local, remote], context, (0, cells), attend_out, gains[0, 1:2], expand, contract, write)


def window_b_away_kernel(
    window_a_first, notes, taken_side, taken_corner, taken_end, near_query, near_key, near_value,
    gains, attend_in, attend_out, expand, contract,
    away_side, away_corner, home_end, query, key, value, bias, context,
):
    cells = away_side.shape[0]
    skip = 2 * cells
    for near, whole in ((near_query, query), (near_key, key), (near_value, value)):
        whole[pl.ds(0, cells), :] = near[...]
    fields = []
    bands_here = [notes[0:1, skip : skip + cells]]
    masks_here = [notes[1:2, skip : skip + cells]]
    for taken in (taken_end, taken_side, taken_corner):
        fields.append(taken[pl.ds(0, cells), :].astype(F32))
        masks, row_bands = meta_of(taken, cells)
        masks_here.append(masks)
        bands_here.append(row_bands)
    bands_here[2] = bands_here[0]
    project(
        jnp.concatenate(fields, 0), gains[0, 0:1], attend_in,
        ((query, key, value), cells, 3 * cells),
    )
    set_bias(bias, jnp.concatenate(bands_here, 1), jnp.concatenate(masks_here, 1))
    attend(query, key, value, bias, context, cells, 3 * cells)

    def write(index, out):
        out = out.astype(BF16)
        if index == 0:
            away_side[...], away_corner[...] = out[:cells], out[cells:]
        else:
            home_end[...] = out

    fields = [jnp.concatenate(fields[1:], 0), fields[0]]
    finish(fields, context, (2 * cells, cells), attend_out, gains[0, 1:2], expand, contract, write)


def between_kernel(
    cells_here, query, key, value, bias, gains, attend_out, expand, contract,
    home, far, notes, next_gains, attend_in_hbm, attend_out_hbm, expand_hbm, contract_hbm,
    home_side, next_query, next_key, next_value, next_bias,
    next_attend_in, next_attend_out, next_expand, next_contract, context, sems,
):
    loads = (
        (attend_in_hbm, next_attend_in), (attend_out_hbm, next_attend_out),
        (expand_hbm, next_expand), (contract_hbm, next_contract),
    )
    copies = [
        pltpu.make_async_copy(source.at[1], target, sems.at[index])
        for index, (source, target) in enumerate(loads)
    ]
    for copy in copies:
        copy.start()
    part = home_side.shape[0]
    attend(query, key, value, bias, context, 0, part)
    near = cells_here[pl.ds(cells_here.shape[0] - part, part), :]
    kept = []

    def write(index, out):
        home_side[...] = out.astype(BF16)
        kept.append(out.astype(BF16).astype(F32))

    finish([near.astype(F32)], context, (0,), attend_out, gains[0, 1:2], expand, contract, write)
    for index in range(2):
        set_bias(next_bias.at[index], notes[2 * index + 2 : 2 * index + 3],
                 notes[2 * index + 3 : 2 * index + 4])
    copies[0].wait()
    windows = [(next_query.at[at], next_key.at[at], next_value.at[at]) for at in range(2)]
    field = [home[:part], far[:part], home[part:]]
    field = [piece.astype(F32) for piece in field] + [kept[0], far[part:].astype(F32)]
    project(
        jnp.concatenate(field, 0), next_gains[1, 0:1], next_attend_in,
        (windows[0], part, part), (windows[0], 3 * part, part), (windows[1], 0, 3 * part),
    )
    for copy in copies[1:]:
        copy.wait()


def second_kernel(
    home, home_side, far, far_side, far_corner, near_end,
    early_query, early_key, early_value, bias,
    gains, attend_in, attend_out, expand, contract,
    out_hbm, query, key, value, context, out_ref, sems,
):
    part = SH * SW
    copies = []
    low, high = slice(0, part), slice(part, 2 * part)
    windows = (
        (near_end[...], home[low], far_corner[...], far[low]),
        (home[high], home_side[...], far[high], far_side[...]),
    )
    windows = [[piece.astype(F32) for piece in parts] for parts in windows]
    refs = [(query.at[at], key.at[at], value.at[at]) for at in range(2)]
    project(
        jnp.concatenate([windows[0][0], windows[0][2], windows[1][3]], 0),
        gains[1, 0:1], attend_in,
        (refs[0], 0, part), (refs[0], 2 * part, part), (refs[1], 3 * part, part),
    )
    fields = [jnp.concatenate(parts[at : at + 2], 0) for parts in windows for at in (0, 2)]
    near = {}

    def write(index, out):
        window = index // 2
        if index % 2 == 0:
            near[window] = out
            return
        both = [piece.reshape(WH, SW, D) for piece in (out, near.pop(window))]
        rows = pl.ds(window * WH, WH)
        out_ref[rows] = jnp.concatenate(both, 1).astype(BF16)
        copies.append(pltpu.make_async_copy(out_ref.at[rows], out_hbm.at[rows], sems.at[window]))
        copies[-1].start()

    def look(index, between=()):
        attend(
            query.at[index], key.at[index], value.at[index], bias.at[index],
            context.at[pl.ds(4 * part * index, 4 * part)], 0, 4 * part, between,
        )

    def rest(first):
        lows = [2 * part * at for at in (first, first + 1)]
        return finish_steps(
            fields[first : first + 2], context, lows, attend_out, gains[1, 1:2], expand, contract,
            lambda index, out: write(first + index, out),
        )

    look(0)
    look(1, rest(0))
    for step in rest(2):
        step()
    for copy in copies:
        copy.wait()


def call(kernel, name, shapes, specs, scratch, flops, *operands, limit=32, aliases=(), outs=VMEM):
    size = sum(operand.size * operand.dtype.itemsize for operand in operands)
    shapes = [shape if isinstance(shape, jax.ShapeDtypeStruct) else jax.ShapeDtypeStruct(shape, BF16)
              for shape in shapes]
    return pl.pallas_call(
        kernel,
        out_shape=shapes,
        in_specs=specs,
        out_specs=[outs] + [VMEM] * (len(shapes) - 1),
        scratch_shapes=scratch,
        compiler_params=pltpu.CompilerParams(vmem_limit_bytes=limit * 2**20),
        cost_estimate=pl.CostEstimate(flops=flops, bytes_accessed=size, transcendentals=0),
        input_output_aliases=dict(aliases),
        name=name,
    )(*operands)


def on_device(
    atmosphere, pole_band, key_valid, norm_gains, attend_in, attend_out, expand, contract
):
    height, breadth = atmosphere.shape[0], atmosphere.shape[1]
    assert height == 2 * WH and breadth == WW
    lons, lats = lax.axis_size("lon"), lax.axis_size("lat")

    def moved(value, lon_step, lat_step):
        pairs = [
            (lon * lats + lat, (lon + lon_step) % lons * lats + (lat + lat_step) % lats)
            for lon in range(lons)
            for lat in range(lats)
        ]
        return lax.ppermute(value, ("lon", "lat"), pairs)

    cells = WH * WW
    half, quarter = cells // 2, cells // 4
    wide = pltpu.VMEM((cells, D), BF16)
    bias_shape = jax.ShapeDtypeStruct((cells, cells), F32)
    bias_scratch = pltpu.VMEM((cells, cells), F32)
    hidden = expand.shape[-1]
    each = 2 * D * 3 * D
    flops = cells * 2 * D * (D + 2 * hidden) + 4 * cells * cells * D

    valid = key_valid.T
    valid_scratch = pltpu.VMEM(valid.shape, valid.dtype)
    main, token = call(
        pack_main_kernel, "pack_main", [(half + META, D), (META, 2 * HD)], [HBM] * 2,
        [pltpu.VMEM((WH, breadth, D), BF16), valid_scratch, pltpu.SemaphoreType.DMA((2,))],
        10**6, atmosphere, valid, limit=62,
    )
    far_main = moved(main, -1, 0)

    weights = [
        (norm_gains, attend_in[0], attend_out[0], expand[0], contract[0]),
        (norm_gains, attend_in, attend_out, expand, contract),
    ]
    side, corner, row_end, here, *prepared = call(
        early_kernel, "early",
        [(quarter + META, D)] * 3 + [(half + quarter, D)] + [(quarter, D)] * 3
        + [jax.ShapeDtypeStruct((META, D), F32)] + [(cells, D)] * 3 + [bias_shape],
        [VMEM, SMEM] + [VMEM] * 4, [], each * (half + quarter),
        atmosphere, pole_band, valid, token, *weights[0][:2],
    )
    near, notes, first = prepared[:3], prepared[3], prepared[4:]
    far_side = moved(side, -1, 0)
    far_corner = moved(corner, -1, -1)
    near_end = moved(row_end, 0, -1)

    away, home, *_ = call(
        window_a_kernel, "window_a", [(half, D)] * 2 + [(cells, D)] * 3 + [bias_shape],
        [VMEM] * 11, [wide], flops + each * half,
        here, far_main, *first, *weights[0],
        aliases=((2, 2), (3, 3), (4, 4), (5, 5)),
    )
    back_main = moved(away, 1, 0)
    away_side, away_corner, home_end, *inside = call(
        window_b_away_kernel, "window_b_away",
        [(quarter, D)] * 3 + [(cells, D)] * 3 + [bias_shape], [VMEM] * 13,
        [wide], 3 * flops // 4 + each * 3 * quarter,
        home, notes, far_side, far_corner, near_end, *near, *weights[0],
    )
    pair = (2, cells, D)
    home_side, *inside = call(
        between_kernel, "between",
        [(quarter, D)] + [pair] * 3 + [jax.ShapeDtypeStruct((2, cells, cells), F32)]
        + [array.shape[1:] for array in weights[1][1:]],
        [VMEM] * 13 + [HBM] * 4, [wide, pltpu.SemaphoreType.DMA((4,))], flops // 4 + each * 5 * quarter,
        here, *inside, weights[0][0], *weights[0][2:],
        home, back_main, notes, *weights[1],
    )
    back_side = moved(away_side, 1, 0)
    back_corner = moved(away_corner, 1, 1)
    back_end = moved(home_end, 0, 1)
    return call(
        second_kernel, "second", [(height, breadth, D)] + [pair] * 3, [VMEM] * 15,
        [pltpu.VMEM((2 * cells, D), BF16), pltpu.VMEM(atmosphere.shape, BF16),
         pltpu.SemaphoreType.DMA((2,))],
        2 * flops + each * 5 * quarter,
        home, home_side, back_main, back_side, back_corner, back_end, *inside[:4], norm_gains, *inside[4:],
        aliases=((6, 1), (7, 2), (8, 3)), outs=HBM,
    )[0]


def solution(mesh):
    in_specs = (
        P(("groups", "lat"), "lon", None),
        P(("groups", "lat")),
        P(("groups", "lat"), "lon"),
        P(),
        P(),
        P(),
        P(),
        P(),
    )
    out_specs = P(("groups", "lat"), "lon", None)
    return jax.shard_map(
        on_device, mesh=mesh, in_specs=in_specs, out_specs=out_specs, check_vma=False
    )
```

```python
import functools
import math

import jax
import jax.numpy as jnp
from jax import lax
from jax.experimental import pallas as pl
from jax.experimental.pallas import tpu as pltpu
from jax.sharding import PartitionSpec as P

D = 512
H = 8
WH = 32
WW = 16
HD = 64
SH = 16
SW = 8

norm_eps = 1e-05

F32 = jnp.float32
BF16 = jnp.bfloat16
CLASSES = 128
META = 16
QSCALE = math.log2(math.e) / math.sqrt(HD)
TRANSPOSED_RIGHT = (((1,), (1,)), ((), ()))
TRANSPOSED_LEFT = (((0,), (0,)), ((), ()))
VMEM = pl.BlockSpec(memory_space=pltpu.VMEM)
SMEM = pl.BlockSpec(memory_space=pltpu.SMEM)
HBM = pl.BlockSpec(memory_space=pltpu.HBM)


def product(left, right):
    return jnp.dot(left, right, preferred_element_type=F32)


def normalize(field, gains):
    average = jnp.mean(field, -1, keepdims=True)
    centred = field - average
    spread = jnp.mean(centred * centred, -1, keepdims=True)
    return (centred * lax.rsqrt(spread + norm_eps) * gains).astype(BF16)


def gelu(value):
    scale = math.sqrt(2.0 / math.pi)
    bent = jnp.tanh(value * (scale + (scale * 0.044715) * (value * value)))
    half = 0.5 * value
    return half + half * bent


def half_columns(block, start):
    part = block.astype(F32)[:, start : start + SW]
    return part.reshape(block.shape[0] * SW, D)


def mask_lanes(valid, low, start, lanes):
    columns, height = valid.shape
    row = lax.broadcasted_iota(jnp.int32, (height, lanes), 0)
    cell = lax.broadcasted_iota(jnp.int32, (height, lanes), 1)
    pick = (row == low + lax.div(cell, SW)).astype(F32).astype(BF16)
    spread = product(valid[...].astype(F32).astype(BF16), pick)
    column = lax.broadcasted_iota(jnp.int32, (columns, lanes), 0)
    own = start + lax.rem(lax.broadcasted_iota(jnp.int32, (columns, lanes), 1), SW)
    return jnp.sum(jnp.where(column == own, spread, 0.0), 0, keepdims=True)


def band_lanes(bands, start, rows, lanes):
    own = lax.div(lax.broadcasted_iota(jnp.int32, (1, lanes), 1), SW)
    found = jnp.zeros((1, lanes), jnp.int32)
    for row in range(rows):
        found = jnp.where(own == row, bands[start + row], found)
    return found.astype(F32)


def meta_rows(masks, bands):
    row = lax.broadcasted_iota(jnp.int32, (META, masks.shape[1]), 0)
    return jnp.where(row == 0, masks, jnp.where(row == 1, bands, 0.0)).astype(BF16)


def meta_of(ref, cells):
    tail = ref[pl.ds(cells, META), :].astype(F32)
    return tail[0:1, :cells], tail[1:2, :cells]


def in_turn(count, stages):
    state = [None] * count
    for step in range(count + len(stages) - 1):
        for index, stage in enumerate(stages):
            piece = step - index
            if 0 <= piece < count:
                state[piece] = stage(piece, state[piece])


def project(field, gain, attend_in, *places):
    normed = normalize(field, gain)
    for kind in range(3):
        result = product(normed, attend_in[:, kind * D : (kind + 1) * D])
        result = (result * QSCALE if kind == 0 else result).astype(BF16)
        done = 0
        for refs, at, count in places:
            refs[kind][pl.ds(at, count), :] = result[done : done + count]
            done += count


def set_bias(bias, bands, masks):
    cells = bands.shape[1]
    classes = lax.broadcasted_iota(jnp.int32, (CLASSES, cells), 0).astype(F32)
    one_hot = (classes == bands).astype(F32).astype(BF16)
    same = lax.dot_general(one_hot, one_hot, TRANSPOSED_LEFT, preferred_element_type=F32)
    asking = lax.broadcasted_iota(jnp.int32, (cells, cells), 0)
    asked = lax.broadcasted_iota(jnp.int32, (cells, cells), 1)
    allowed = (same > 0.5) & ((masks > 0.5) | (asking == asked))
    bias[...] = jnp.where(allowed, 0.0, -1e30)


def attend(query, key, value, bias, context, low, count):
    attend_windows([(query, key, value, bias, context)], low, count)


def attend_windows(windows, low, count):
    first = lax.broadcasted_iota(jnp.int32, (1, 2 * HD), 1) < HD
    rows = pl.ds(low, count)
    sums = {}

    def lanes(unit):
        return slice(2 * HD * (unit % H // 2), 2 * HD * (unit % H // 2 + 1))

    def own(unit, inside, outside):
        return jnp.where(first, inside, outside) if unit % 2 == 0 else jnp.where(first, outside, inside)

    def score(unit, _):
        query, key, _, bias, _ = windows[unit // H]
        queries = query[rows, lanes(unit)]
        queries = own(unit, queries, jnp.zeros_like(queries))
        scores = lax.dot_general(
            queries, key[:, lanes(unit)], TRANSPOSED_RIGHT, preferred_element_type=F32
        )
        return scores + bias[rows, :]

    def weigh(unit, scores):
        return jnp.exp2(scores - jnp.max(scores, -1, keepdims=True)).astype(BF16)

    def gather(unit, weights):
        _, _, value, _, context = windows[unit // H]
        values = value[:, lanes(unit)]
        sums[unit] = product(weights, own(unit, values, jnp.ones_like(values)))
        if unit % 2 == 1:
            even, odd = sums.pop(unit - 1), sums.pop(unit)
            above = jnp.where(first, even, odd)
            below = pltpu.roll(jnp.where(first, odd, even), HD, 1)
            context[rows, lanes(unit)] = (above / below).astype(BF16)

    in_turn(len(windows) * H, (score, weigh, gather))


def finish(fields, context, lows, attend_out, gain, expand, contract, write):
    def start(index, _):
        rows = pl.ds(lows[index], fields[index].shape[0])
        added = fields[index] + product(context[rows, :], attend_out[...])
        resid = added.astype(BF16).astype(F32)
        return resid, normalize(resid, gain)

    def widen(index, state):
        return state[0], product(state[1], expand[...])

    def bend(index, state):
        return state[0], gelu(state[1]).astype(BF16)

    def end(index, state):
        write(index, state[0] + product(state[1], contract[...]))

    in_turn(len(fields), (start, widen, bend, end))


def pack_main_kernel(block_hbm, valid_hbm, main, token, block, valid, sems):
    height = block_hbm.shape[0]
    rows = height - 2 * SH
    copies = (
        pltpu.make_async_copy(valid_hbm, valid, sems.at[0]),
        pltpu.make_async_copy(block_hbm.at[pl.ds(SH, rows)], block, sems.at[1]),
    )
    for copy in copies:
        copy.start()
    token[...] = jnp.zeros_like(token)
    copies[0].wait()
    masks = mask_lanes(valid, SH, 0, D)
    main[pl.ds(rows * SW, META), :] = meta_rows(masks, jnp.zeros_like(masks))
    copies[1].wait()
    main[pl.ds(0, rows * SW), :] = half_columns(block[...], 0).astype(BF16)


def early_kernel(
    block, bands, valid, token, gains, attend_in,
    side, corner, row_end, cells_here, query, key, value, notes,
):
    height = block.shape[0]
    part = SH * SW
    for out, low, column in ((side, height - SH, 0), (corner, 0, 0), (row_end, 0, SW)):
        out[pl.ds(0, part), :] = half_columns(block[low : low + SH], column).astype(BF16)
        masks = mask_lanes(valid, low, column, D)
        out[pl.ds(part, META), :] = meta_rows(masks, band_lanes(bands, low, SH, D))
    local = half_columns(block[SH:], SW)
    cells_here[...] = local.astype(BF16)
    window_notes = [
        (band_lanes(bands, SH, height - SH, D), mask_lanes(valid, SH, SW, D)),
    ]
    for row in range(0, height, WH):
        row_bands = band_lanes(bands, row, WH, 2 * part)
        window_notes.append((
            jnp.concatenate([row_bands, row_bands], 1),
            jnp.concatenate(
                [mask_lanes(valid, row, SW, 2 * part), mask_lanes(valid, row, 0, 2 * part)], 1
            ),
        ))
    for index, pair in enumerate(window_notes):
        for offset, lanes in enumerate(pair):
            notes[pl.ds(2 * index + offset, 1), :] = lanes
    project(local, gains[0, 0:1], attend_in, ((query, key, value), 0, local.shape[0]))


def window_a_kernel(
    cells_here, notes, taken, near_query, near_key, near_value,
    gains, attend_in, attend_out, expand, contract,
    away, home, query, key, value, bias, context,
):
    cells = away.shape[0]
    for near, whole in ((near_query, query), (near_key, key), (near_value, value)):
        whole[pl.ds(0, cells), :] = near[pl.ds(0, cells), :]
    local = cells_here[pl.ds(0, cells), :].astype(F32)
    remote = taken[pl.ds(0, cells), :].astype(F32)
    project(remote, gains[0, 0:1], attend_in, ((query, key, value), cells, cells))
    row_bands = notes[0:1, :cells]
    masks, _ = meta_of(taken, cells)
    set_bias(
        bias,
        jnp.concatenate([row_bands, row_bands], 1),
        jnp.concatenate([notes[1:2, :cells], masks], 1),
    )
    attend(query, key, value, bias, context, 0, 2 * cells)

    def write(index, out):
        (home, away)[index][...] = out.astype(BF16)

    finish([local, remote], context, (0, cells), attend_out, gains[0, 1:2], expand, contract, write)


def window_b_away_kernel(
    window_a_first, notes, taken_side, taken_corner, taken_end, near_query, near_key, near_value,
    gains, attend_in, attend_out, expand, contract,
    away_side, away_corner, home_end, query, key, value, bias, context,
):
    cells = away_side.shape[0]
    skip = near_query.shape[0] - cells
    for near, whole in ((near_query, query), (near_key, key), (near_value, value)):
        whole[pl.ds(0, cells), :] = near[pl.ds(skip, cells), :]
    fields = []
    bands_here = [notes[0:1, skip : skip + cells]]
    masks_here = [notes[1:2, skip : skip + cells]]
    for taken in (taken_end, taken_side, taken_corner):
        fields.append(taken[pl.ds(0, cells), :].astype(F32))
        masks, row_bands = meta_of(taken, cells)
        masks_here.append(masks)
        bands_here.append(row_bands)
    bands_here[2] = bands_here[0]
    project(
        jnp.concatenate(fields, 0), gains[0, 0:1], attend_in,
        ((query, key, value), cells, 3 * cells),
    )
    set_bias(bias, jnp.concatenate(bands_here, 1), jnp.concatenate(masks_here, 1))
    attend(query, key, value, bias, context, cells, 3 * cells)

    def write(index, out):
        out = out.astype(BF16)
        if index == 0:
            away_side[...], away_corner[...] = out[:cells], out[cells:]
        else:
            home_end[...] = out

    fields = [jnp.concatenate(fields[1:], 0), fields[0]]
    finish(fields, context, (2 * cells, cells), attend_out, gains[0, 1:2], expand, contract, write)


def between_kernel(
    cells_here, query, key, value, bias, gains, attend_out, expand, contract,
    home, far, notes, next_gains, attend_in_hbm, attend_out_hbm, expand_hbm, contract_hbm,
    home_side, next_query, next_key, next_value, next_bias,
    next_attend_in, next_attend_out, next_expand, next_contract, context, sems,
):
    loads = (
        (attend_in_hbm, next_attend_in), (attend_out_hbm, next_attend_out),
        (expand_hbm, next_expand), (contract_hbm, next_contract),
    )
    copies = [
        pltpu.make_async_copy(source.at[1], target, sems.at[index])
        for index, (source, target) in enumerate(loads)
    ]
    for copy in copies:
        copy.start()
    part = home_side.shape[0]
    attend(query, key, value, bias, context, 0, part)
    near = cells_here[pl.ds(cells_here.shape[0] - part, part), :]
    kept = []

    def write(index, out):
        home_side[...] = out.astype(BF16)
        kept.append(out.astype(BF16).astype(F32))

    finish([near.astype(F32)], context, (0,), attend_out, gains[0, 1:2], expand, contract, write)
    for index in range(2):
        set_bias(next_bias.at[index], notes[2 * index + 2 : 2 * index + 3],
                 notes[2 * index + 3 : 2 * index + 4])
    copies[0].wait()
    windows = [(next_query.at[at], next_key.at[at], next_value.at[at]) for at in range(2)]
    field = [home[:part], far[:part], home[part:]]
    field = [piece.astype(F32) for piece in field] + [kept[0], far[part:].astype(F32)]
    project(
        jnp.concatenate(field, 0), next_gains[1, 0:1], next_attend_in,
        (windows[0], part, part), (windows[0], 3 * part, part), (windows[1], 0, 3 * part),
    )
    for copy in copies[1:]:
        copy.wait()


def second_kernel(
    home, home_side, far, far_side, far_corner, near_end,
    early_query, early_key, early_value, bias,
    gains, attend_in, attend_out, expand, contract,
    out_hbm, query, key, value, context, out_ref, sems,
):
    part = SH * SW
    copies = []
    low, high = slice(0, part), slice(part, 2 * part)
    windows = (
        (near_end[...], home[low], far_corner[...], far[low]),
        (home[high], home_side[...], far[high], far_side[...]),
    )
    windows = [[piece.astype(F32) for piece in parts] for parts in windows]
    refs = [(query.at[at], key.at[at], value.at[at]) for at in range(2)]
    project(
        jnp.concatenate([windows[0][0], windows[0][2], windows[1][3]], 0),
        gains[1, 0:1], attend_in,
        (refs[0], 0, part), (refs[0], 2 * part, part), (refs[1], 3 * part, part),
    )
    attend_windows(
        [
            (*refs[at], bias.at[at], context.at[pl.ds(4 * part * at, 4 * part)])
            for at in range(len(windows))
        ],
        0, 4 * part,
    )
    fields = [jnp.concatenate(parts[at : at + 2], 0) for parts in windows for at in (0, 2)]
    near = {}

    def write(index, out):
        window = index // 2
        if index % 2 == 0:
            near[window] = out
            return
        both = [piece.reshape(WH, SW, D) for piece in (out, near.pop(window))]
        rows = pl.ds(window * WH, WH)
        out_ref[rows] = jnp.concatenate(both, 1).astype(BF16)
        copies.append(pltpu.make_async_copy(out_ref.at[rows], out_hbm.at[rows], sems.at[window]))
        copies[-1].start()

    lows = [2 * part * at for at in range(len(fields))]
    finish(fields, context, lows, attend_out, gains[1, 1:2], expand, contract, write)
    for copy in copies:
        copy.wait()


def call(kernel, name, shapes, specs, scratch, flops, *operands, limit=32, aliases=(), outs=VMEM):
    size = sum(operand.size * operand.dtype.itemsize for operand in operands)
    shapes = [shape if isinstance(shape, jax.ShapeDtypeStruct) else jax.ShapeDtypeStruct(shape, BF16)
              for shape in shapes]
    return pl.pallas_call(
        kernel,
        out_shape=shapes,
        in_specs=specs,
        out_specs=[outs] + [VMEM] * (len(shapes) - 1),
        scratch_shapes=scratch,
        compiler_params=pltpu.CompilerParams(vmem_limit_bytes=limit * 2**20),
        cost_estimate=pl.CostEstimate(flops=flops, bytes_accessed=size, transcendentals=0),
        input_output_aliases=dict(aliases),
        name=name,
    )(*operands)


def on_device(
    atmosphere, pole_band, key_valid, norm_gains, attend_in, attend_out, expand, contract
):
    height, breadth = atmosphere.shape[0], atmosphere.shape[1]
    assert height == 2 * WH and breadth == WW
    lons, lats = lax.axis_size("lon"), lax.axis_size("lat")

    def moved(value, lon_step, lat_step):
        pairs = [
            (lon * lats + lat, (lon + lon_step) % lons * lats + (lat + lat_step) % lats)
            for lon in range(lons)
            for lat in range(lats)
        ]
        return lax.ppermute(value, ("lon", "lat"), pairs)

    cells = WH * WW
    half, quarter = cells // 2, cells // 4
    wide = pltpu.VMEM((cells, D), BF16)
    bias_shape = jax.ShapeDtypeStruct((cells, cells), F32)
    bias_scratch = pltpu.VMEM((cells, cells), F32)
    hidden = expand.shape[-1]
    each = 2 * D * 3 * D
    flops = cells * 2 * D * (D + 2 * hidden) + 4 * cells * cells * D

    valid = key_valid.T
    valid_scratch = pltpu.VMEM(valid.shape, valid.dtype)
    main, token = call(
        pack_main_kernel, "pack_main", [(half + META, D), (META, 2 * HD)], [HBM] * 2,
        [pltpu.VMEM((WH, breadth, D), BF16), valid_scratch, pltpu.SemaphoreType.DMA((2,))],
        10**6, atmosphere, valid, limit=62,
    )
    far_main = moved(main, -1, 0)

    weights = [
        (norm_gains, attend_in[0], attend_out[0], expand[0], contract[0]),
        (norm_gains, attend_in, attend_out, expand, contract),
    ]
    side, corner, row_end, here, *near, notes = call(
        early_kernel, "early",
        [(quarter + META, D)] * 3 + [(half + quarter, D)] * 4
        + [jax.ShapeDtypeStruct((META, D), F32)],
        [VMEM, SMEM] + [VMEM] * 4, [], each * (half + quarter),
        atmosphere, pole_band, valid, token, *weights[0][:2],
    )
    far_side = moved(side, -1, 0)
    far_corner = moved(corner, -1, -1)
    near_end = moved(row_end, 0, -1)

    away, home = call(
        window_a_kernel, "window_a", [(half, D)] * 2, [VMEM] * 11,
        [wide] * 3 + [bias_scratch, wide], flops + each * half,
        here, notes, far_main, *near, *weights[0],
    )
    back_main = moved(away, 1, 0)
    away_side, away_corner, home_end, *inside = call(
        window_b_away_kernel, "window_b_away",
        [(quarter, D)] * 3 + [(cells, D)] * 3 + [bias_shape], [VMEM] * 13,
        [wide], 3 * flops // 4 + each * 3 * quarter,
        home, notes, far_side, far_corner, near_end, *near, *weights[0],
    )
    pair = (2, cells, D)
    home_side, *inside = call(
        between_kernel, "between",
        [(quarter, D)] + [pair] * 3 + [jax.ShapeDtypeStruct((2, cells, cells), F32)]
        + [array.shape[1:] for array in weights[1][1:]],
        [VMEM] * 13 + [HBM] * 4, [wide, pltpu.SemaphoreType.DMA((4,))], flops // 4 + each * 5 * quarter,
        here, *inside, weights[0][0], *weights[0][2:],
        home, back_main, notes, *weights[1],
    )
    back_side = moved(away_side, 1, 0)
    back_corner = moved(away_corner, 1, 1)
    back_end = moved(home_end, 0, 1)
    return call(
        second_kernel, "second", [(height, breadth, D)] + [pair] * 3, [VMEM] * 15,
        [pltpu.VMEM((2 * cells, D), BF16), pltpu.VMEM(atmosphere.shape, BF16),
         pltpu.SemaphoreType.DMA((2,))],
        2 * flops + each * 5 * quarter,
        home, home_side, back_main, back_side, back_corner, back_end, *inside[:4], norm_gains, *inside[4:],
        aliases=((6, 1), (7, 2), (8, 3)), outs=HBM,
    )[0]


def solution(mesh):
    in_specs = (
        P(("groups", "lat"), "lon", None),
        P(("groups", "lat")),
        P(("groups", "lat"), "lon"),
        P(),
        P(),
        P(),
        P(),
        P(),
    )
    out_specs = P(("groups", "lat"), "lon", None)
    return jax.shard_map(
        on_device, mesh=mesh, in_specs=in_specs, out_specs=out_specs, check_vma=False
    )
```

```python
import functools
import math

import jax
import jax.numpy as jnp
from jax import lax
from jax.experimental import pallas as pl
from jax.experimental.pallas import tpu as pltpu
from jax.sharding import PartitionSpec as P

D = 512
H = 8
WH = 32
WW = 16
HD = 64
SH = 16
SW = 8

norm_eps = 1e-05

F32 = jnp.float32
BF16 = jnp.bfloat16
CLASSES = 128
META = 16
QSCALE = math.log2(math.e) / math.sqrt(HD)
TRANSPOSED_RIGHT = (((1,), (1,)), ((), ()))
TRANSPOSED_LEFT = (((0,), (0,)), ((), ()))
VMEM = pl.BlockSpec(memory_space=pltpu.VMEM)
SMEM = pl.BlockSpec(memory_space=pltpu.SMEM)
HBM = pl.BlockSpec(memory_space=pltpu.HBM)


def product(left, right):
    return jnp.dot(left, right, preferred_element_type=F32)


def normalize(field, gains):
    average = jnp.mean(field, -1, keepdims=True)
    centred = field - average
    spread = jnp.mean(centred * centred, -1, keepdims=True)
    return (centred * lax.rsqrt(spread + norm_eps) * gains).astype(BF16)


def gelu(value):
    scale = math.sqrt(2.0 / math.pi)
    bent = jnp.tanh(value * (scale + (scale * 0.044715) * (value * value)))
    half = 0.5 * value
    return half + half * bent


def half_columns(block, start):
    part = block.astype(F32)[:, start : start + SW]
    return part.reshape(block.shape[0] * SW, D)


def mask_lanes(valid, low, start, lanes):
    columns, height = valid.shape
    row = lax.broadcasted_iota(jnp.int32, (height, lanes), 0)
    cell = lax.broadcasted_iota(jnp.int32, (height, lanes), 1)
    pick = (row == low + lax.div(cell, SW)).astype(F32).astype(BF16)
    spread = product(valid[...].astype(F32).astype(BF16), pick)
    column = lax.broadcasted_iota(jnp.int32, (columns, lanes), 0)
    own = start + lax.rem(lax.broadcasted_iota(jnp.int32, (columns, lanes), 1), SW)
    return jnp.sum(jnp.where(column == own, spread, 0.0), 0, keepdims=True)


def band_lanes(bands, start, rows, lanes):
    own = lax.div(lax.broadcasted_iota(jnp.int32, (1, lanes), 1), SW)
    found = jnp.zeros((1, lanes), jnp.int32)
    for row in range(rows):
        found = jnp.where(own == row, bands[start + row], found)
    return found.astype(F32)


def meta_rows(masks, bands):
    row = lax.broadcasted_iota(jnp.int32, (META, masks.shape[1]), 0)
    return jnp.where(row == 0, masks, jnp.where(row == 1, bands, 0.0)).astype(BF16)


def meta_of(ref, cells):
    tail = ref[pl.ds(cells, META), :].astype(F32)
    return tail[0:1, :cells], tail[1:2, :cells]


def in_turn(count, stages):
    state = [None] * count
    for step in range(count + len(stages) - 1):
        for index, stage in enumerate(stages):
            piece = step - index
            if 0 <= piece < count:
                state[piece] = stage(piece, state[piece])


def project(field, gain, attend_in, *places):
    normed = normalize(field, gain)
    for kind in range(3):
        result = product(normed, attend_in[:, kind * D : (kind + 1) * D])
        result = (result * QSCALE if kind == 0 else result).astype(BF16)
        done = 0
        for refs, at, count in places:
            refs[kind][pl.ds(at, count), :] = result[done : done + count]
            done += count


def set_bias(bias, bands, masks):
    cells = bands.shape[1]
    classes = lax.broadcasted_iota(jnp.int32, (CLASSES, cells), 0).astype(F32)
    one_hot = (classes == bands).astype(F32).astype(BF16)
    same = lax.dot_general(one_hot, one_hot, TRANSPOSED_LEFT, preferred_element_type=F32)
    asking = lax.broadcasted_iota(jnp.int32, (cells, cells), 0)
    asked = lax.broadcasted_iota(jnp.int32, (cells, cells), 1)
    allowed = (same > 0.5) & ((masks > 0.5) | (asking == asked))
    bias[...] = jnp.where(allowed, 0.0, -1e30)


def attend(query, key, value, bias, context, low, count):
    attend_windows([(query, key, value, bias, context)], low, count)


def attend_windows(windows, low, count):
    first = lax.broadcasted_iota(jnp.int32, (1, 2 * HD), 1) < HD
    rows = pl.ds(low, count)
    sums = {}

    def lanes(unit):
        return slice(2 * HD * (unit % H // 2), 2 * HD * (unit % H // 2 + 1))

    def own(unit, inside, outside):
        return jnp.where(first, inside, outside) if unit % 2 == 0 else jnp.where(first, outside, inside)

    def score(unit, _):
        query, key, _, bias, _ = windows[unit // H]
        queries = query[rows, lanes(unit)]
        queries = own(unit, queries, jnp.zeros_like(queries))
        scores = lax.dot_general(
            queries, key[:, lanes(unit)], TRANSPOSED_RIGHT, preferred_element_type=F32
        )
        return scores + bias[rows, :]

    def weigh(unit, scores):
        return jnp.exp2(scores - jnp.max(scores, -1, keepdims=True)).astype(BF16)

    def gather(unit, weights):
        _, _, value, _, context = windows[unit // H]
        values = value[:, lanes(unit)]
        sums[unit] = product(weights, own(unit, values, jnp.ones_like(values)))
        if unit % 2 == 1:
            even, odd = sums.pop(unit - 1), sums.pop(unit)
            above = jnp.where(first, even, odd)
            below = pltpu.roll(jnp.where(first, odd, even), HD, 1)
            context[rows, lanes(unit)] = (above / below).astype(BF16)

    in_turn(len(windows) * H, (score, weigh, gather))


def finish(fields, context, lows, attend_out, gain, expand, contract, write):
    def start(index, _):
        rows = pl.ds(lows[index], fields[index].shape[0])
        added = fields[index] + product(context[rows, :], attend_out[...])
        resid = added.astype(BF16).astype(F32)
        return resid, normalize(resid, gain)

    def widen(index, state):
        return state[0], product(state[1], expand[...])

    def bend(index, state):
        return state[0], gelu(state[1]).astype(BF16)

    def end(index, state):
        write(index, state[0] + product(state[1], contract[...]))

    in_turn(len(fields), (start, widen, bend, end))


def pack_main_kernel(block_hbm, valid_hbm, main, token, block, valid, sems):
    height = block_hbm.shape[0]
    rows = height - 2 * SH
    copies = (
        pltpu.make_async_copy(valid_hbm, valid, sems.at[0]),
        pltpu.make_async_copy(block_hbm.at[pl.ds(SH, rows)], block, sems.at[1]),
    )
    for copy in copies:
        copy.start()
    token[...] = jnp.zeros_like(token)
    copies[0].wait()
    masks = mask_lanes(valid, SH, 0, D)
    main[pl.ds(rows * SW, META), :] = meta_rows(masks, jnp.zeros_like(masks))
    copies[1].wait()
    main[pl.ds(0, rows * SW), :] = half_columns(block[...], 0).astype(BF16)


def early_kernel(
    block, bands, valid, token, gains, attend_in,
    side, corner, row_end, cells_here, query, key, value, notes,
):
    height = block.shape[0]
    part = SH * SW
    for out, low, column in ((side, height - SH, 0), (corner, 0, 0), (row_end, 0, SW)):
        out[pl.ds(0, part), :] = half_columns(block[low : low + SH], column).astype(BF16)
        masks = mask_lanes(valid, low, column, D)
        out[pl.ds(part, META), :] = meta_rows(masks, band_lanes(bands, low, SH, D))
    local = half_columns(block[SH:], SW)
    cells_here[...] = local.astype(BF16)
    window_notes = [
        (band_lanes(bands, SH, height - SH, D), mask_lanes(valid, SH, SW, D)),
    ]
    for row in range(0, height, WH):
        row_bands = band_lanes(bands, row, WH, 2 * part)
        window_notes.append((
            jnp.concatenate([row_bands, row_bands], 1),
            jnp.concatenate(
                [mask_lanes(valid, row, SW, 2 * part), mask_lanes(valid, row, 0, 2 * part)], 1
            ),
        ))
    for index, pair in enumerate(window_notes):
        for offset, lanes in enumerate(pair):
            notes[pl.ds(2 * index + offset, 1), :] = lanes
    project(local, gains[0, 0:1], attend_in, ((query, key, value), 0, local.shape[0]))


def window_a_kernel(
    cells_here, notes, taken, near_query, near_key, near_value,
    gains, attend_in, attend_out, expand, contract,
    away, home, query, key, value, bias, context,
):
    cells = away.shape[0]
    for near, whole in ((near_query, query), (near_key, key), (near_value, value)):
        whole[pl.ds(0, cells), :] = near[pl.ds(0, cells), :]
    local = cells_here[pl.ds(0, cells), :].astype(F32)
    remote = taken[pl.ds(0, cells), :].astype(F32)
    project(remote, gains[0, 0:1], attend_in, ((query, key, value), cells, cells))
    row_bands = notes[0:1, :cells]
    masks, _ = meta_of(taken, cells)
    set_bias(
        bias,
        jnp.concatenate([row_bands, row_bands], 1),
        jnp.concatenate([notes[1:2, :cells], masks], 1),
    )
    attend(query, key, value, bias, context, 0, 2 * cells)

    def write(index, out):
        (home, away)[index][...] = out.astype(BF16)

    finish([local, remote], context, (0, cells), attend_out, gains[0, 1:2], expand, contract, write)


def window_b_away_kernel(
    window_a_first, notes, taken_side, taken_corner, taken_end, near_query, near_key, near_value,
    gains, attend_in, attend_out, expand, contract,
    away_side, away_corner, home_end, query, key, value, bias, context,
):
    cells = away_side.shape[0]
    skip = near_query.shape[0] - cells
    for near, whole in ((near_query, query), (near_key, key), (near_value, value)):
        whole[pl.ds(0, cells), :] = near[pl.ds(skip, cells), :]
    fields = []
    bands_here = [notes[0:1, skip : skip + cells]]
    masks_here = [notes[1:2, skip : skip + cells]]
    for taken in (taken_end, taken_side, taken_corner):
        fields.append(taken[pl.ds(0, cells), :].astype(F32))
        masks, row_bands = meta_of(taken, cells)
        masks_here.append(masks)
        bands_here.append(row_bands)
    bands_here[2] = bands_here[0]
    project(
        jnp.concatenate(fields, 0), gains[0, 0:1], attend_in,
        ((query, key, value), cells, 3 * cells),
    )
    set_bias(bias, jnp.concatenate(bands_here, 1), jnp.concatenate(masks_here, 1))
    attend(query, key, value, bias, context, cells, 3 * cells)

    def write(index, out):
        out = out.astype(BF16)
        if index == 0:
            away_side[...], away_corner[...] = out[:cells], out[cells:]
        else:
            home_end[...] = out

    fields = [jnp.concatenate(fields[1:], 0), fields[0]]
    finish(fields, context, (2 * cells, cells), attend_out, gains[0, 1:2], expand, contract, write)


def between_kernel(
    cells_here, query, key, value, bias, gains, attend_out, expand, contract,
    home, far, notes, next_gains, attend_in_hbm, attend_out_hbm, expand_hbm, contract_hbm,
    home_side, next_query, next_key, next_value, next_bias,
    next_attend_in, next_attend_out, next_expand, next_contract, context, sems,
):
    loads = (
        (attend_in_hbm, next_attend_in), (attend_out_hbm, next_attend_out),
        (expand_hbm, next_expand), (contract_hbm, next_contract),
    )
    copies = [
        pltpu.make_async_copy(source.at[1], target, sems.at[index])
        for index, (source, target) in enumerate(loads)
    ]
    for copy in copies:
        copy.start()
    part = home_side.shape[0]
    attend(query, key, value, bias, context, 0, part)
    near = cells_here[pl.ds(cells_here.shape[0] - part, part), :]
    kept = []

    def write(index, out):
        home_side[...] = out.astype(BF16)
        kept.append(out.astype(BF16).astype(F32))

    finish([near.astype(F32)], context, (0,), attend_out, gains[0, 1:2], expand, contract, write)
    for index in range(2):
        set_bias(next_bias.at[index], notes[2 * index + 2 : 2 * index + 3],
                 notes[2 * index + 3 : 2 * index + 4])
    copies[0].wait()
    windows = [(next_query.at[at], next_key.at[at], next_value.at[at]) for at in range(2)]
    field = [home[:part], far[:part], home[part:]]
    field = [piece.astype(F32) for piece in field] + [kept[0], far[part:].astype(F32)]
    project(
        jnp.concatenate(field, 0), next_gains[1, 0:1], next_attend_in,
        (windows[0], part, part), (windows[0], 3 * part, part), (windows[1], 0, 3 * part),
    )
    for copy in copies[1:]:
        copy.wait()


def second_kernel(
    home, home_side, far, far_side, far_corner, near_end,
    early_query, early_key, early_value, bias,
    gains, attend_in, attend_out, expand, contract,
    out_hbm, query, key, value, context, out_ref, sems,
):
    part = SH * SW
    copies = []
    low, high = slice(0, part), slice(part, 2 * part)
    windows = (
        (near_end[...], home[low], far_corner[...], far[low]),
        (home[high], home_side[...], far[high], far_side[...]),
    )
    windows = [[piece.astype(F32) for piece in parts] for parts in windows]
    refs = [(query.at[at], key.at[at], value.at[at]) for at in range(2)]
    project(
        jnp.concatenate([windows[0][0], windows[0][2], windows[1][3]], 0),
        gains[1, 0:1], attend_in,
        (refs[0], 0, part), (refs[0], 2 * part, part), (refs[1], 3 * part, part),
    )
    attend_windows(
        [
            (*refs[at], bias.at[at], context.at[pl.ds(4 * part * at, 4 * part)])
            for at in range(len(windows))
        ],
        0, 4 * part,
    )
    fields = [jnp.concatenate(parts, 0) for parts in windows]

    def write(window, out):
        rows = pl.ds(window * WH, WH)
        both = [out[at : at + 2 * part].reshape(WH, SW, D) for at in (2 * part, 0)]
        out_ref[rows] = jnp.concatenate(both, 1).astype(BF16)
        copies.append(pltpu.make_async_copy(out_ref.at[rows], out_hbm.at[rows], sems.at[window]))
        copies[-1].start()

    lows = [4 * part * at for at in range(len(fields))]
    finish(fields, context, lows, attend_out, gains[1, 1:2], expand, contract, write)
    for copy in copies:
        copy.wait()


def call(kernel, name, shapes, specs, scratch, flops, *operands, limit=32, aliases=(), outs=VMEM):
    size = sum(operand.size * operand.dtype.itemsize for operand in operands)
    shapes = [shape if isinstance(shape, jax.ShapeDtypeStruct) else jax.ShapeDtypeStruct(shape, BF16)
              for shape in shapes]
    return pl.pallas_call(
        kernel,
        out_shape=shapes,
        in_specs=specs,
        out_specs=[outs] + [VMEM] * (len(shapes) - 1),
        scratch_shapes=scratch,
        compiler_params=pltpu.CompilerParams(vmem_limit_bytes=limit * 2**20),
        cost_estimate=pl.CostEstimate(flops=flops, bytes_accessed=size, transcendentals=0),
        input_output_aliases=dict(aliases),
        name=name,
    )(*operands)


def on_device(
    atmosphere, pole_band, key_valid, norm_gains, attend_in, attend_out, expand, contract
):
    height, breadth = atmosphere.shape[0], atmosphere.shape[1]
    assert height == 2 * WH and breadth == WW
    lons, lats = lax.axis_size("lon"), lax.axis_size("lat")

    def moved(value, lon_step, lat_step):
        pairs = [
            (lon * lats + lat, (lon + lon_step) % lons * lats + (lat + lat_step) % lats)
            for lon in range(lons)
            for lat in range(lats)
        ]
        return lax.ppermute(value, ("lon", "lat"), pairs)

    cells = WH * WW
    half, quarter = cells // 2, cells // 4
    wide = pltpu.VMEM((cells, D), BF16)
    bias_shape = jax.ShapeDtypeStruct((cells, cells), F32)
    bias_scratch = pltpu.VMEM((cells, cells), F32)
    hidden = expand.shape[-1]
    each = 2 * D * 3 * D
    flops = cells * 2 * D * (D + 2 * hidden) + 4 * cells * cells * D

    valid = key_valid.T
    valid_scratch = pltpu.VMEM(valid.shape, valid.dtype)
    main, token = call(
        pack_main_kernel, "pack_main", [(half + META, D), (META, 2 * HD)], [HBM] * 2,
        [pltpu.VMEM((WH, breadth, D), BF16), valid_scratch, pltpu.SemaphoreType.DMA((2,))],
        10**6, atmosphere, valid, limit=62,
    )
    far_main = moved(main, -1, 0)

    weights = [
        (norm_gains, attend_in[0], attend_out[0], expand[0], contract[0]),
        (norm_gains, attend_in, attend_out, expand, contract),
    ]
    side, corner, row_end, here, *near, notes = call(
        early_kernel, "early",
        [(quarter + META, D)] * 3 + [(half + quarter, D)] * 4
        + [jax.ShapeDtypeStruct((META, D), F32)],
        [VMEM, SMEM] + [VMEM] * 4, [], each * (half + quarter),
        atmosphere, pole_band, valid, token, *weights[0][:2],
    )
    far_side = moved(side, -1, 0)
    far_corner = moved(corner, -1, -1)
    near_end = moved(row_end, 0, -1)

    away, home = call(
        window_a_kernel, "window_a", [(half, D)] * 2, [VMEM] * 11,
        [wide] * 3 + [bias_scratch, wide], flops + each * half,
        here, notes, far_main, *near, *weights[0],
    )
    back_main = moved(away, 1, 0)
    away_side, away_corner, home_end, *inside = call(
        window_b_away_kernel, "window_b_away",
        [(quarter, D)] * 3 + [(cells, D)] * 3 + [bias_shape], [VMEM] * 13,
        [wide], 3 * flops // 4 + each * 3 * quarter,
        home, notes, far_side, far_corner, near_end, *near, *weights[0],
    )
    pair = (2, cells, D)
    home_side, *inside = call(
        between_kernel, "between",
        [(quarter, D)] + [pair] * 3 + [jax.ShapeDtypeStruct((2, cells, cells), F32)]
        + [array.shape[1:] for array in weights[1][1:]],
        [VMEM] * 13 + [HBM] * 4, [wide, pltpu.SemaphoreType.DMA((4,))], flops // 4 + each * 5 * quarter,
        here, *inside, weights[0][0], *weights[0][2:],
        home, back_main, notes, *weights[1],
    )
    back_side = moved(away_side, 1, 0)
    back_corner = moved(away_corner, 1, 1)
    back_end = moved(home_end, 0, 1)
    return call(
        second_kernel, "second", [(height, breadth, D)] + [pair] * 3, [VMEM] * 15,
        [pltpu.VMEM((2 * cells, D), BF16), pltpu.VMEM(atmosphere.shape, BF16),
         pltpu.SemaphoreType.DMA((2,))],
        2 * flops + each * 5 * quarter,
        home, home_side, back_main, back_side, back_corner, back_end, *inside[:4], norm_gains, *inside[4:],
        aliases=((6, 1), (7, 2), (8, 3)), outs=HBM,
    )[0]


def solution(mesh):
    in_specs = (
        P(("groups", "lat"), "lon", None),
        P(("groups", "lat")),
        P(("groups", "lat"), "lon"),
        P(),
        P(),
        P(),
        P(),
        P(),
    )
    out_specs = P(("groups", "lat"), "lon", None)
    return jax.shard_map(
        on_device, mesh=mesh, in_specs=in_specs, out_specs=out_specs, check_vma=False
    )
```
